32 devices in a mesh: grp: 2 (over y), tm: 8 (over z, x), chan: 2 (over core).
Axes of the slice: x: 2, y: 2, z: 4, core: 2. Of those that a mesh axis runs over, the one named last changes fastest.
Arguments:
- signal: bfloat16 [8192, 1024], P(('grp', 'tm'), 'chan'), parts along dimension 0, may hold values from -6 to 6
- filter_weight: bfloat16 [3, 1024, 1024], P(None, 'tm', 'chan'), may hold values from -0.109375 to 0.109375
- gate_weight: bfloat16 [3, 1024, 1024], P(None, 'tm', 'chan'), may hold values from -0.109375 to 0.109375
- filter_bias: float32 [1024], P('chan'), may hold values from -3 to 3
- gate_bias: float32 [1024], P('chan'), may hold values from -3 to 3
- mix_weight: bfloat16 [1024, 1024], P('chan', 'tm'), may hold values from -0.1875 to 0.1875
- cotangent: bfloat16 [8192, 1024], P(('grp', 'tm'), 'chan'), parts along dimension 0, may hold values from -6 to 6
Outputs:
- output: bfloat16 [8192, 1024], P(('grp', 'tm'), 'chan'), parts along dimension 0
- input_grad: bfloat16 [8192, 1024], P(('grp', 'tm'), 'chan'), parts along dimension 0
The draws below stay inside these ranges and needn't reach their ends.
There are 2 independent parts, one for each index of `grp`. The reference program is written for one: setup_inputs(seed, part) draws one part's arguments, and reference() takes and returns one part's arrays. A program takes and returns all parts, laid end to end along the dimension named above; an argument that names none is the same for every part. Nothing has to cross between parts.
All inputs are finite; a program needn't handle non-finite values.
Results may differ from the reference program's by a relative error of at most 0.006.
Values may be sent and summed in bfloat16 or wider, within the bound.
A program may use at most 64 MiB of HBM per device.

```python
import jax
import jax.numpy as jnp

C = 1024
H = 1024
KERNEL_TAPS = 3
DILATION_STEPS = 512
TOKENS = 4096


def levels(own_key, extent, shards, smallest, largest):
    factor_of = 1.0
    for position, blocks in shards:
        heights = jax.random.uniform(jax.random.fold_in(jax.random.fold_in(own_key, 6), position), (blocks,), jnp.float32, smallest / len(shards), largest / len(shards))
        factor_of = factor_of * jnp.repeat(jnp.exp(heights), extent[position] // blocks).reshape((-1,) + (1,) * (len(extent) - 1 - position))
    return factor_of


def centred(key, extent, deviation, bound, split=(), kind=jnp.bfloat16):
    factor_of = levels(key, extent, split, -0.22, 0.18) if split else 1.0
    array = jax.random.normal(key, extent, jnp.float32) * deviation * factor_of
    return jnp.minimum(jnp.maximum(array, -bound), bound).astype(kind)


def setup_inputs(seed: int = 0, part: int = 0) -> dict:
    keys = jax.random.split(jax.random.key(seed), 8)
    own_keys = jax.random.split(jax.random.fold_in(keys[7], part), 8)
    return {
        "signal": centred(own_keys[0], (TOKENS, C), 1.0, 6.0, ((0, 8), (1, 2))),
        "filter_weight": centred(keys[1], (KERNEL_TAPS, C, H), (KERNEL_TAPS * C) ** -0.5, 0.109375, ((1, 8), (2, 2))),
        "gate_weight": centred(keys[2], (KERNEL_TAPS, C, H), (KERNEL_TAPS * C) ** -0.5, 0.109375, ((1, 8), (2, 2))),
        "filter_bias": centred(keys[3], (H,), 0.5, 3.0, ((0, 2),), jnp.float32),
        "gate_bias": centred(keys[4], (H,), 0.5, 3.0, ((0, 2),), jnp.float32),
        "mix_weight": centred(keys[5], (H, C), H ** -0.5, 0.1875, ((0, 2), (1, 8))),
        "cotangent": centred(own_keys[6], (TOKENS, C), 1.0, 6.0, ((0, 8), (1, 2))),
    }


def reference(signal, filter_weight, gate_weight, filter_bias, gate_bias, mix_weight, cotangent):
    receptive_rows = (KERNEL_TAPS - 1) * DILATION_STEPS
    sequence_length = signal.shape[0]
    padded_input = jnp.concatenate([jnp.zeros((receptive_rows, C), signal.dtype), signal], axis=0)
    sum_filter = jnp.zeros((sequence_length, H), jnp.float32)
    sum_gate = jnp.zeros((sequence_length, H), jnp.float32)
    for tap_position in range(KERNEL_TAPS):
        first_row_index = receptive_rows - tap_position * DILATION_STEPS
        lagged = padded_input[first_row_index:first_row_index + sequence_length]
        sum_filter = sum_filter + jnp.dot(lagged, filter_weight[tap_position], preferred_element_type=jnp.float32)
        sum_gate = sum_gate + jnp.dot(lagged, gate_weight[tap_position], preferred_element_type=jnp.float32)
    pre_filter = sum_filter + filter_bias
    pre_gate = sum_gate + gate_bias
    tangent = jnp.tanh(pre_filter)
    opened = jax.nn.sigmoid(pre_gate)
    hidden = (tangent * opened).astype(jnp.bfloat16)
    output = (signal.astype(jnp.float32) + jnp.dot(hidden, mix_weight, preferred_element_type=jnp.float32)).astype(jnp.bfloat16)
    back_hidden = jnp.dot(cotangent, mix_weight.T, preferred_element_type=jnp.float32)
    grad_filter = (back_hidden * opened * (1.0 - tangent * tangent)).astype(jnp.bfloat16)
    grad_gate = (back_hidden * tangent * opened * (1.0 - opened)).astype(jnp.bfloat16)
    after_filter = jnp.concatenate([grad_filter, jnp.zeros((receptive_rows, H), grad_filter.dtype)], axis=0)
    after_gate = jnp.concatenate([grad_gate, jnp.zeros((receptive_rows, H), grad_gate.dtype)], axis=0)
    total = cotangent.astype(jnp.float32)
    for tap_position in range(KERNEL_TAPS):
        first_row_index = tap_position * DILATION_STEPS
        total = total + jnp.dot(after_filter[first_row_index:first_row_index + sequence_length], filter_weight[tap_position].T, preferred_element_type=jnp.float32)
        total = total + jnp.dot(after_gate[first_row_index:first_row_index + sequence_length], gate_weight[tap_position].T, preferred_element_type=jnp.float32)
    return output, total.astype(jnp.bfloat16)
```

```python
import jax
import jax.numpy as jnp
from jax import lax
from jax.experimental import pallas as pl
from jax.experimental.pallas import tpu as pltpu
from jax.sharding import PartitionSpec as P

KERNEL_TAPS = 3
DILATION_STEPS = 512


def shifted(value, axis, steps):
    count = lax.axis_size(axis)
    leading, last = (max(0, -steps), min(count, count - steps))
    return lax.ppermute(value, axis, [(source, source + steps) for source in range(leading, last)])


def fetch_before(block, receptive_rows):
    sequence_length = block.shape[0]
    hop_count = -(-receptive_rows // sequence_length)
    pieces = []
    for hop_index in range(1, hop_count + 1):
        pieces.insert(0, shifted(block, "tm", hop_index))
    joined = jnp.concatenate(pieces, axis=0)
    return joined


def fetch_after(block, receptive_rows):
    sequence_length = block.shape[0]
    hop_count = -(-receptive_rows // sequence_length)
    pieces = []
    for hop_index in range(1, hop_count + 1):
        pieces.append(shifted(block, "tm", -hop_index))
    joined = jnp.concatenate(pieces, axis=0)
    return joined


def per_device(signal, filter_weight, gate_weight, filter_bias, gate_bias, mix_weight, cotangent):
    sequence_length = signal.shape[0]
    receptive_rows = (KERNEL_TAPS - 1) * DILATION_STEPS
    filter_full, gate_full, mix_full = (
        lax.all_gather(filter_weight, "tm", axis=1, tiled=True),
        lax.all_gather(gate_weight, "tm", axis=1, tiled=True),
        lax.all_gather(mix_weight, "tm", axis=1, tiled=True),
    )
    half_hidden = filter_full.shape[2]
    stacked = jnp.concatenate([filter_full, gate_full], axis=2)
    whole = lax.all_gather(signal, "chan", axis=1, tiled=True)
    earlier = fetch_before(whole, receptive_rows)
    padded_input = jnp.concatenate([earlier, whole], axis=0)
    lagged = jnp.concatenate(
        [
            padded_input[
                receptive_rows
                - tap_position * DILATION_STEPS : receptive_rows
                - tap_position * DILATION_STEPS
                + sequence_length
            ]
            for tap_position in range(KERNEL_TAPS)
        ],
        axis=1,
    )
    bias_both = jnp.concatenate([filter_bias, gate_bias])
    pre_both = (
        jnp.dot(lagged, stacked.reshape(-1, stacked.shape[2]), preferred_element_type=jnp.float32)
        + bias_both
    )
    tangent = jnp.tanh(pre_both[:, :half_hidden])
    opened = jax.nn.sigmoid(pre_both[:, half_hidden:])
    hidden = (tangent * opened).astype(jnp.bfloat16)
    mixed = lax.psum_scatter(
        jnp.dot(hidden, mix_full, preferred_element_type=jnp.float32).astype(jnp.bfloat16),
        "chan",
        scatter_dimension=1,
        tiled=True,
    ).astype(jnp.float32)
    output = (signal.astype(jnp.float32) + mixed).astype(jnp.bfloat16)
    cot_whole = lax.all_gather(cotangent, "chan", axis=1, tiled=True)
    back_hidden = lax.dot_general(
        cot_whole, mix_full, (((1,), (1,)), ((), ())), preferred_element_type=jnp.float32
    )
    grad_filter = (back_hidden * opened * (1.0 - tangent * tangent)).astype(jnp.bfloat16)
    grad_gate = (back_hidden * tangent * opened * (1.0 - opened)).astype(jnp.bfloat16)
    grad_both = jnp.concatenate([grad_filter, grad_gate], axis=1)
    later = fetch_after(grad_both, receptive_rows)
    forward_rows = jnp.concatenate([grad_both, later], axis=0)
    total = jnp.zeros((sequence_length, stacked.shape[1]), jnp.float32)
    for tap_position in range(KERNEL_TAPS):
        input_window = forward_rows[
            tap_position * DILATION_STEPS : tap_position * DILATION_STEPS + sequence_length
        ]
        total = total + lax.dot_general(
            input_window,
            stacked[tap_position],
            (((1,), (1,)), ((), ())),
            preferred_element_type=jnp.float32,
        )
    input_part = lax.psum_scatter(
        total.astype(jnp.bfloat16), "chan", scatter_dimension=1, tiled=True
    ).astype(jnp.float32)
    input_grad = (cotangent.astype(jnp.float32) + input_part).astype(jnp.bfloat16)
    return (output, input_grad)

F32 = jnp.float32
BF16 = jnp.bfloat16
NT = (((1,), (1,)), ((), ()))
DEPTH = 4
TILE = 256


def fused_kernel(
    signal_ref, filter_ref, gate_ref, fbias_ref, gbias_ref, mixw_ref, cot_ref,
    out_ref, ig_ref,
    w, mix, sig, cot, grads, hidden, keep, xout, xin, qout, rin,
    wsend, wrecv, msend, mrecv, ssend, srecv, fsend, frecv, csend, crecv,
    xsend, xrecv, qsend, qrecv, local,
):
    grp, tm, chan = lax.axis_index("grp"), lax.axis_index("tm"), lax.axis_index("chan")
    z, x = tm // 2, tm % 2
    rows = filter_ref.shape[1]
    half = cot_ref.shape[1]
    last = 2 * DEPTH - 1
    circ = (grp + chan) % 2
    other = 1 - circ
    here = chan * half
    there = (1 - chan) * half

    up, down = (grp, tm + 2, chan), (grp, tm - 2, chan)
    side, twin, mate = (grp, tm + 1 - 2 * x, chan), (1 - grp, tm, chan), (grp, tm, 1 - chan)
    has_up, has_down = z < DEPTH - 1, z > 0
    corner_at = tm - 1 + 2 * x
    has_corner = jnp.logical_and(corner_at >= 0, corner_at <= last)

    def lanes(start, size):
        return pl.ds(pl.multiple_of(start, 128), size)

    def remote(src, dst, send, recv, to):
        return pltpu.make_async_remote_copy(
            src_ref=src, dst_ref=dst, send_sem=send, recv_sem=recv,
            device_id=to, device_id_type=pl.DeviceIdType.MESH,
        )

    own_copies = [
        pltpu.make_async_copy(filter_ref, w.at[0, :, lanes(tm * rows, rows), :], local.at[0]),
        pltpu.make_async_copy(gate_ref, w.at[1, :, lanes(tm * rows, rows), :], local.at[1]),
        pltpu.make_async_copy(mixw_ref, mix.at[:, lanes(tm * rows, rows)], local.at[2]),
        pltpu.make_async_copy(signal_ref, sig.at[0, :, lanes(here, half)], local.at[3]),
        pltpu.make_async_copy(cot_ref, cot.at[:, lanes(here, half)], local.at[4]),
    ]
    for copy in own_copies:
        copy.start()

    barrier = pltpu.get_barrier_semaphore()

    def greet(to):
        pl.semaphore_signal(barrier, inc=1, device_id=to, device_id_type=pl.DeviceIdType.MESH)

    greet(side)
    greet(twin)
    greet(mate)
    pl.when(has_up)(lambda: greet(up))
    pl.when(has_down)(lambda: greet(down))
    pl.when(has_corner)(lambda: greet((grp, corner_at, chan)))
    pl.semaphore_wait(
        barrier,
        3 + has_up.astype(jnp.int32) + has_down.astype(jnp.int32) + has_corner.astype(jnp.int32),
    )

    def halo(lag):
        return remote(
            sig.at[0, :, lanes(here, half)], sig.at[lag, :, lanes(here, half)],
            ssend.at[lag], srecv.at[lag], (grp, tm + lag, chan),
        )

    def to_mate(lag, columns):
        return remote(
            sig.at[lag, :, lanes(columns, half)], sig.at[lag, :, lanes(columns, half)],
            fsend.at[lag], frecv.at[lag], mate,
        )

    def cot_copy(columns):
        return remote(
            cot.at[:, lanes(columns, half)], cot.at[:, lanes(columns, half)],
            csend.at[0], crecv.at[0], mate,
        )

    peers = (up, down, side, twin)

    def piece(array, tap, shard, way):
        slot = w.at[array, tap, lanes(shard * rows, rows), :]
        return remote(slot, slot, wsend.at[way, tap, shard], wrecv.at[array, tap, shard], peers[way])

    def mix_piece(shard, way):
        slot = mix.at[:, lanes(shard * rows, rows)]
        return remote(slot, slot, msend.at[way, shard], mrecv.at[shard], peers[way])

    def each_tap(body):
        lax.fori_loop(0, KERNEL_TAPS, lambda tap, c: (body(tap), c)[1], 0)

    def ring_round(step, make, act, arrive, hand_over):
        if step == 0:
            pl.when(has_up)(lambda: act(make(tm, 0)))
            pl.when(has_down)(lambda: act(make(tm, 1)))
            act(make(tm, 2))
            return

        @pl.when(z >= step)
        def _():
            shard = tm - 2 * step
            arrive(make(shard, 2))
            pl.when(has_up)(lambda: act(make(shard, 0)))
            act(make(shard, 2))
            if hand_over:
                act(make(shard, 3))

        @pl.when(z + step < DEPTH)
        def _():
            shard = tm + 2 * step
            arrive(make(shard, 2))
            pl.when(has_down)(lambda: act(make(shard, 1)))
            act(make(shard, 2))
            if hand_over:
                act(make(shard, 3))

    def side_round(step, make, act, arrive, hand_over):
        def one(shard):
            arrive(make(shard, 2))
            if hand_over:
                act(make(shard, 3))

        base = tm + 1 - 2 * x
        if step == 0:
            one(base)
            return
        pl.when(z >= step)(lambda: one(base - 2 * step))
        pl.when(z + step < DEPTH)(lambda: one(base + 2 * step))

    start = lambda copy: copy.start()
    sent = lambda copy: copy.wait_send()
    landed = lambda copy: copy.wait_recv()
    skip = lambda copy: None

    def w_make(tap):
        return lambda shard, way: piece(circ, tap, shard, way)

    own_copies[3].wait()
    for lag in (1, 2):
        pl.when(tm + lag <= last)(lambda: halo(lag).start())
    own_copies[2].wait()
    ring_round(0, mix_piece, start, landed, False)
    own_copies[0].wait()
    own_copies[1].wait()
    each_tap(lambda tap: ring_round(0, w_make(tap), start, landed, True))
    to_mate(0, here).start()
    own_copies[4].wait()
    cot_copy(here).start()

    for lag in (1, 2):
        @pl.when(tm < lag)
        def _():
            sig[lag] = jnp.zeros_like(sig[lag])

        @pl.when(tm + lag > last)
        def _():
            rin[lag - 1] = jnp.zeros_like(rin[lag - 1])

    for step in range(1, DEPTH):
        ring_round(step, mix_piece, start, landed, False)
        side_round(step - 1, mix_piece, start, landed, False)

        def body(tap):
            ring_round(step, w_make(tap), start, landed, True)
            side_round(step - 1, w_make(tap), start, landed, True)

        each_tap(body)
        if step < 3:
            @pl.when(tm >= step)
            def _():
                halo(step).wait_recv()
                to_mate(step, here).start()
    side_round(DEPTH - 1, mix_piece, start, landed, False)
    each_tap(lambda tap: side_round(DEPTH - 1, w_make(tap), start, landed, True))

    to_mate(0, there).wait_recv()
    for lag in (1, 2):
        pl.when(tm >= lag)(lambda: to_mate(lag, there).wait_recv())
    cot_copy(there).wait_recv()

    def other_landed(tap):
        def one(step, c):
            piece(other, tap, (tm + step) % (last + 1), 3).wait_recv()
            return c

        lax.fori_loop(1, last + 1, one, 0)

    each_tap(other_landed)

    def tiles(body):
        def one(i, c):
            body(pl.multiple_of(i * TILE, TILE))
            return c

        lax.fori_loop(0, half // TILE, one, 0)

    def forward(col):
        columns = pl.ds(col, TILE)
        pre_f = jnp.broadcast_to(fbias_ref[:, columns], (sig.shape[1], TILE))
        pre_g = jnp.broadcast_to(gbias_ref[:, columns], (sig.shape[1], TILE))
        for tap in range(KERNEL_TAPS):
            pre_f += jnp.dot(sig[tap], w[0, tap, :, columns], preferred_element_type=F32)
            pre_g += jnp.dot(sig[tap], w[1, tap, :, columns], preferred_element_type=F32)
        t = jnp.tanh(pre_f)
        s = jax.nn.sigmoid(pre_g)
        ts = t * s
        hidden[:, columns] = ts.astype(BF16)
        back = lax.dot_general(cot[...], mix[columns, :], NT, preferred_element_type=F32)
        grads[:, columns] = (back * s * (1.0 - t * t)).astype(BF16)
        grads[:, pl.ds(pl.multiple_of(half + col, TILE), TILE)] = (back * ts * (1.0 - s)).astype(BF16)

    tiles(forward)

    def grad_part(tap, base, col):
        channels = pl.ds(pl.multiple_of(base + col, TILE), TILE)
        return lax.dot_general(
            grads[:, :half], w[0, tap, channels, :], NT, preferred_element_type=F32
        ) + lax.dot_general(grads[:, half:], w[1, tap, channels, :], NT, preferred_element_type=F32)

    def mix_part(base, col):
        channels = pl.ds(pl.multiple_of(base + col, TILE), TILE)
        return jnp.dot(hidden[...], mix[:, channels], preferred_element_type=F32)

    def swap(slot):
        return remote(xout.at[slot], xin.at[slot], xsend.at[slot], xrecv.at[slot], mate)

    def back_copy(tap):
        return remote(
            qout.at[tap - 1], rin.at[tap - 1], qsend.at[tap - 1], qrecv.at[tap - 1], (grp, tm - tap, chan)
        )

    def give(slot, part):
        def one(col):
            xout[slot, :, pl.ds(col, TILE)] = part(there, col).astype(BF16)

        tiles(one)
        swap(slot).start()

    def tap_part(tap):
        return lambda base, col: grad_part(tap, base, col)

    for tap in (2, 1):
        give(tap, tap_part(tap))
    for tap in (2, 1):
        def one(col):
            keep[:, pl.ds(col, TILE)] = grad_part(tap, here, col)

        tiles(one)
        swap(tap).wait_recv()
        qout[tap - 1] = (keep[...] + xin[tap].astype(F32)).astype(BF16)
        pl.when(tm >= tap)(lambda: back_copy(tap).start())
    give(3, mix_part)
    give(0, tap_part(0))

    def out_tile(col):
        keep[:, pl.ds(col, TILE)] = mix_part(here, col)

    tiles(out_tile)
    swap(3).wait_recv()
    out_ref[...] = (
        sig[0, :, lanes(here, half)].astype(F32) + (keep[...] + xin[3].astype(F32))
    ).astype(BF16)

    def ig_tile(col):
        keep[:, pl.ds(col, TILE)] = grad_part(0, here, col)

    tiles(ig_tile)
    swap(0).wait_recv()
    keep[...] = keep[...] + xin[0].astype(F32) + cot[:, lanes(here, half)].astype(F32)
    for tap in (1, 2):
        pl.when(tm + tap <= last)(lambda: back_copy(tap).wait_recv())
    ig_ref[...] = (keep[...] + rin[0].astype(F32) + rin[1].astype(F32)).astype(BF16)

    for lag in (1, 2):
        pl.when(tm + lag <= last)(lambda: halo(lag).wait_send())
        pl.when(tm >= lag)(lambda: to_mate(lag, here).wait_send())
        pl.when(tm >= lag)(lambda: back_copy(lag).wait_send())
    to_mate(0, here).wait_send()
    cot_copy(here).wait_send()
    for slot in range(4):
        swap(slot).wait_send()

    for step in range(DEPTH):
        ring_round(step, mix_piece, sent, skip, False)

    def drain(tap):
        for step in range(DEPTH):
            ring_round(step, w_make(tap), sent, skip, True)
            side_round(step, w_make(tap), sent, skip, True)

    each_tap(drain)


def fused_device(signal, filter_weight, gate_weight, filter_bias, gate_bias, mix_weight, cotangent):
    steps, half = signal.shape
    hid = filter_weight.shape[2]
    count = lax.axis_size("tm")
    width = count * filter_weight.shape[1]
    anywhere = pl.BlockSpec(memory_space=pl.ANY)
    vmem = pl.BlockSpec(memory_space=pltpu.VMEM)
    dma = pltpu.SemaphoreType.DMA
    return pl.pallas_call(
        fused_kernel,
        out_shape=(
            jax.ShapeDtypeStruct((steps, half), BF16),
            jax.ShapeDtypeStruct((steps, half), BF16),
        ),
        in_specs=[anywhere, anywhere, anywhere, vmem, vmem, anywhere, anywhere],
        out_specs=(vmem, vmem),
        scratch_shapes=[
            pltpu.VMEM((2, KERNEL_TAPS, width, hid), BF16),
            pltpu.VMEM((hid, width), BF16),
            pltpu.VMEM((KERNEL_TAPS, steps, width), BF16),
            pltpu.VMEM((steps, width), BF16),
            pltpu.VMEM((steps, 2 * hid), BF16),
            pltpu.VMEM((steps, hid), BF16),
            pltpu.VMEM((steps, half), F32),
            pltpu.VMEM((4, steps, half), BF16),
            pltpu.VMEM((4, steps, half), BF16),
            pltpu.VMEM((2, steps, half), BF16),
            pltpu.VMEM((2, steps, half), BF16),
            dma((4, KERNEL_TAPS, count)),
            dma((2, KERNEL_TAPS, count)),
            dma((3, count)),
            dma((count,)),
            dma((3,)),
            dma((3,)),
            dma((3,)),
            dma((3,)),
            dma((1,)),
            dma((1,)),
            dma((4,)),
            dma((4,)),
            dma((2,)),
            dma((2,)),
            dma((5,)),
        ],
        compiler_params=pltpu.CompilerParams(
            collective_id=0, has_side_effects=True, vmem_limit_bytes=56 * 1024 * 1024
        ),
    )(
        signal, filter_weight, gate_weight, filter_bias.reshape(1, -1), gate_bias.reshape(1, -1),
        mix_weight, cotangent,
    )


def solution(mesh):
    in_specs = (
        P(("grp", "tm"), "chan"),
        P(None, "tm", "chan"),
        P(None, "tm", "chan"),
        P("chan"),
        P("chan"),
        P("chan", "tm"),
        P(("grp", "tm"), "chan"),
    )
    out_specs = (P(("grp", "tm"), "chan"), P(("grp", "tm"), "chan"))
    fits = mesh.shape["tm"] == 2 * DEPTH and mesh.shape["grp"] == 2 and mesh.shape["chan"] == 2
    return jax.shard_map(
        fused_device if fits else per_device, mesh=mesh, in_specs=in_specs, out_specs=out_specs, check_vma=False
    )
```

```python
import jax
import jax.numpy as jnp
from jax import lax
from jax.experimental import pallas as pl
from jax.experimental.pallas import tpu as pltpu
from jax.sharding import PartitionSpec as P

KERNEL_TAPS = 3
DILATION_STEPS = 512


def shifted(value, axis, steps):
    count = lax.axis_size(axis)
    leading, last = (max(0, -steps), min(count, count - steps))
    return lax.ppermute(value, axis, [(source, source + steps) for source in range(leading, last)])


def fetch_before(block, receptive_rows):
    sequence_length = block.shape[0]
    hop_count = -(-receptive_rows // sequence_length)
    pieces = []
    for hop_index in range(1, hop_count + 1):
        pieces.insert(0, shifted(block, "tm", hop_index))
    joined = jnp.concatenate(pieces, axis=0)
    return joined


def fetch_after(block, receptive_rows):
    sequence_length = block.shape[0]
    hop_count = -(-receptive_rows // sequence_length)
    pieces = []
    for hop_index in range(1, hop_count + 1):
        pieces.append(shifted(block, "tm", -hop_index))
    joined = jnp.concatenate(pieces, axis=0)
    return joined


def per_device(signal, filter_weight, gate_weight, filter_bias, gate_bias, mix_weight, cotangent):
    sequence_length = signal.shape[0]
    receptive_rows = (KERNEL_TAPS - 1) * DILATION_STEPS
    filter_full, gate_full, mix_full = (
        lax.all_gather(filter_weight, "tm", axis=1, tiled=True),
        lax.all_gather(gate_weight, "tm", axis=1, tiled=True),
        lax.all_gather(mix_weight, "tm", axis=1, tiled=True),
    )
    half_hidden = filter_full.shape[2]
    stacked = jnp.concatenate([filter_full, gate_full], axis=2)
    whole = lax.all_gather(signal, "chan", axis=1, tiled=True)
    earlier = fetch_before(whole, receptive_rows)
    padded_input = jnp.concatenate([earlier, whole], axis=0)
    lagged = jnp.concatenate(
        [
            padded_input[
                receptive_rows
                - tap_position * DILATION_STEPS : receptive_rows
                - tap_position * DILATION_STEPS
                + sequence_length
            ]
            for tap_position in range(KERNEL_TAPS)
        ],
        axis=1,
    )
    bias_both = jnp.concatenate([filter_bias, gate_bias])
    pre_both = (
        jnp.dot(lagged, stacked.reshape(-1, stacked.shape[2]), preferred_element_type=jnp.float32)
        + bias_both
    )
    tangent = jnp.tanh(pre_both[:, :half_hidden])
    opened = jax.nn.sigmoid(pre_both[:, half_hidden:])
    hidden = (tangent * opened).astype(jnp.bfloat16)
    mixed = lax.psum_scatter(
        jnp.dot(hidden, mix_full, preferred_element_type=jnp.float32).astype(jnp.bfloat16),
        "chan",
        scatter_dimension=1,
        tiled=True,
    ).astype(jnp.float32)
    output = (signal.astype(jnp.float32) + mixed).astype(jnp.bfloat16)
    cot_whole = lax.all_gather(cotangent, "chan", axis=1, tiled=True)
    back_hidden = lax.dot_general(
        cot_whole, mix_full, (((1,), (1,)), ((), ())), preferred_element_type=jnp.float32
    )
    grad_filter = (back_hidden * opened * (1.0 - tangent * tangent)).astype(jnp.bfloat16)
    grad_gate = (back_hidden * tangent * opened * (1.0 - opened)).astype(jnp.bfloat16)
    grad_both = jnp.concatenate([grad_filter, grad_gate], axis=1)
    later = fetch_after(grad_both, receptive_rows)
    forward_rows = jnp.concatenate([grad_both, later], axis=0)
    total = jnp.zeros((sequence_length, stacked.shape[1]), jnp.float32)
    for tap_position in range(KERNEL_TAPS):
        input_window = forward_rows[
            tap_position * DILATION_STEPS : tap_position * DILATION_STEPS + sequence_length
        ]
        total = total + lax.dot_general(
            input_window,
            stacked[tap_position],
            (((1,), (1,)), ((), ())),
            preferred_element_type=jnp.float32,
        )
    input_part = lax.psum_scatter(
        total.astype(jnp.bfloat16), "chan", scatter_dimension=1, tiled=True
    ).astype(jnp.float32)
    input_grad = (cotangent.astype(jnp.float32) + input_part).astype(jnp.bfloat16)
    return (output, input_grad)

F32 = jnp.float32
BF16 = jnp.bfloat16
NT = (((1,), (1,)), ((), ()))
DEPTH = 4
TILE = 256


def fused_kernel(
    signal_ref, filter_ref, gate_ref, fbias_ref, gbias_ref, mixw_ref, cot_ref,
    out_ref, ig_ref,
    w, mix, sig, cot, grads, hidden, keep, xout, xin, qout, rin,
    wsend, wrecv, msend, mrecv, ssend, srecv, fsend, frecv, csend, crecv,
    xsend, xrecv, qsend, qrecv, local,
):
    grp, tm, chan = lax.axis_index("grp"), lax.axis_index("tm"), lax.axis_index("chan")
    z, x = tm // 2, tm % 2
    rows = filter_ref.shape[1]
    half = cot_ref.shape[1]
    last = 2 * DEPTH - 1
    circ = (grp + chan) % 2
    other = 1 - circ
    here = chan * half
    there = (1 - chan) * half

    up, down = (grp, tm + 2, chan), (grp, tm - 2, chan)
    side, twin, mate = (grp, tm + 1 - 2 * x, chan), (1 - grp, tm, chan), (grp, tm, 1 - chan)
    has_up, has_down = z < DEPTH - 1, z > 0
    corner_at = tm - 1 + 2 * x
    has_corner = jnp.logical_and(corner_at >= 0, corner_at <= last)

    def lanes(start, size):
        return pl.ds(pl.multiple_of(start, 128), size)

    def remote(src, dst, send, recv, to):
        return pltpu.make_async_remote_copy(
            src_ref=src, dst_ref=dst, send_sem=send, recv_sem=recv,
            device_id=to, device_id_type=pl.DeviceIdType.MESH,
        )

    own_copies = [
        pltpu.make_async_copy(filter_ref, w.at[0, :, lanes(tm * rows, rows), :], local.at[0]),
        pltpu.make_async_copy(gate_ref, w.at[1, :, lanes(tm * rows, rows), :], local.at[1]),
        pltpu.make_async_copy(mixw_ref, mix.at[:, lanes(tm * rows, rows)], local.at[2]),
        pltpu.make_async_copy(signal_ref, sig.at[0, :, lanes(here, half)], local.at[3]),
        pltpu.make_async_copy(cot_ref, cot.at[:, lanes(here, half)], local.at[4]),
    ]
    for copy in own_copies:
        copy.start()

    barrier = pltpu.get_barrier_semaphore()

    def greet(to):
        pl.semaphore_signal(barrier, inc=1, device_id=to, device_id_type=pl.DeviceIdType.MESH)

    greet(side)
    greet(twin)
    greet(mate)
    pl.when(has_up)(lambda: greet(up))
    pl.when(has_down)(lambda: greet(down))
    pl.when(has_corner)(lambda: greet((grp, corner_at, chan)))
    pl.semaphore_wait(
        barrier,
        3 + has_up.astype(jnp.int32) + has_down.astype(jnp.int32) + has_corner.astype(jnp.int32),
    )

    def halo(held, lag, to):
        return remote(
            sig.at[held, :, lanes(here, half)], sig.at[lag, :, lanes(here, half)],
            ssend.at[lag], srecv.at[lag], to,
        )

    def to_mate(lag, columns):
        return remote(
            sig.at[lag, :, lanes(columns, half)], sig.at[lag, :, lanes(columns, half)],
            fsend.at[lag], frecv.at[lag], mate,
        )

    def cot_copy(columns):
        return remote(
            cot.at[:, lanes(columns, half)], cot.at[:, lanes(columns, half)],
            csend.at[0], crecv.at[0], mate,
        )

    peers = (up, down, side, twin)

    def piece(array, tap, shard, way):
        slot = w.at[array, tap, lanes(shard * rows, rows), :]
        return remote(slot, slot, wsend.at[way, tap, shard], wrecv.at[array, tap, shard], peers[way])

    def mix_piece(shard, way):
        slot = mix.at[:, lanes(shard * rows, rows)]
        return remote(slot, slot, msend.at[way, shard], mrecv.at[shard], peers[way])

    def each_tap(body):
        lax.fori_loop(0, KERNEL_TAPS, lambda tap, c: (body(tap), c)[1], 0)

    def ring_round(step, make, act, arrive, hand_over):
        if step == 0:
            pl.when(has_up)(lambda: act(make(tm, 0)))
            pl.when(has_down)(lambda: act(make(tm, 1)))
            act(make(tm, 2))
            return

        @pl.when(z >= step)
        def _():
            shard = tm - 2 * step
            arrive(make(shard, 2))
            pl.when(has_up)(lambda: act(make(shard, 0)))
            act(make(shard, 2))
            if hand_over:
                act(make(shard, 3))

        @pl.when(z + step < DEPTH)
        def _():
            shard = tm + 2 * step
            arrive(make(shard, 2))
            pl.when(has_down)(lambda: act(make(shard, 1)))
            act(make(shard, 2))
            if hand_over:
                act(make(shard, 3))

    def side_round(step, make, act, arrive, hand_over):
        def one(shard):
            arrive(make(shard, 2))
            if hand_over:
                act(make(shard, 3))

        base = tm + 1 - 2 * x
        if step == 0:
            one(base)
            return
        pl.when(z >= step)(lambda: one(base - 2 * step))
        pl.when(z + step < DEPTH)(lambda: one(base + 2 * step))

    start = lambda copy: copy.start()
    sent = lambda copy: copy.wait_send()
    landed = lambda copy: copy.wait_recv()
    skip = lambda copy: None

    def w_make(tap):
        return lambda shard, way: piece(circ, tap, shard, way)

    own_copies[3].wait()
    own_copies[2].wait()
    ring_round(0, mix_piece, start, landed, False)
    own_copies[0].wait()
    own_copies[1].wait()
    each_tap(lambda tap: ring_round(0, w_make(tap), start, landed, True))
    pl.when(has_up)(lambda: halo(0, 2, up).start())
    pl.when(x == 0)(lambda: halo(0, 1, side).start())
    to_mate(0, here).start()
    own_copies[4].wait()
    cot_copy(here).start()

    for lag in (1, 2):
        @pl.when(tm < lag)
        def _():
            sig[lag] = jnp.zeros_like(sig[lag])

        @pl.when(tm + lag > last)
        def _():
            rin[lag - 1] = jnp.zeros_like(rin[lag - 1])

    for step in range(1, DEPTH):
        ring_round(step, mix_piece, start, landed, False)
        side_round(step - 1, mix_piece, start, landed, False)

        def body(tap):
            ring_round(step, w_make(tap), start, landed, True)
            side_round(step - 1, w_make(tap), start, landed, True)

        each_tap(body)
        if step == 1:
            @pl.when(has_down)
            def _():
                halo(0, 2, side).wait_recv()
                pl.when(x == 1)(lambda: halo(2, 1, side).start())
                to_mate(2, here).start()

        if step == 2:
            @pl.when(tm >= 1)
            def _():
                halo(0, 1, side).wait_recv()
                to_mate(1, here).start()
    side_round(DEPTH - 1, mix_piece, start, landed, False)
    each_tap(lambda tap: side_round(DEPTH - 1, w_make(tap), start, landed, True))

    to_mate(0, there).wait_recv()
    for lag in (1, 2):
        pl.when(tm >= lag)(lambda: to_mate(lag, there).wait_recv())
    cot_copy(there).wait_recv()

    def other_landed(tap):
        def one(step, c):
            piece(other, tap, (tm + step) % (last + 1), 3).wait_recv()
            return c

        lax.fori_loop(1, last + 1, one, 0)

    each_tap(other_landed)

    def tiles(body):
        def one(i, c):
            body(pl.multiple_of(i * TILE, TILE))
            return c

        lax.fori_loop(0, half // TILE, one, 0)

    def forward(col):
        columns = pl.ds(col, TILE)
        pre_f = jnp.broadcast_to(fbias_ref[:, columns], (sig.shape[1], TILE))
        pre_g = jnp.broadcast_to(gbias_ref[:, columns], (sig.shape[1], TILE))
        for tap in range(KERNEL_TAPS):
            pre_f += jnp.dot(sig[tap], w[0, tap, :, columns], preferred_element_type=F32)
            pre_g += jnp.dot(sig[tap], w[1, tap, :, columns], preferred_element_type=F32)
        t = jnp.tanh(pre_f)
        s = jax.nn.sigmoid(pre_g)
        ts = t * s
        hidden[:, columns] = ts.astype(BF16)
        back = lax.dot_general(cot[...], mix[columns, :], NT, preferred_element_type=F32)
        grads[:, columns] = (back * s * (1.0 - t * t)).astype(BF16)
        grads[:, pl.ds(pl.multiple_of(half + col, TILE), TILE)] = (back * ts * (1.0 - s)).astype(BF16)

    tiles(forward)

    def grad_part(tap, base, col):
        channels = pl.ds(pl.multiple_of(base + col, TILE), TILE)
        return lax.dot_general(
            grads[:, :half], w[0, tap, channels, :], NT, preferred_element_type=F32
        ) + lax.dot_general(grads[:, half:], w[1, tap, channels, :], NT, preferred_element_type=F32)

    def mix_part(base, col):
        channels = pl.ds(pl.multiple_of(base + col, TILE), TILE)
        return jnp.dot(hidden[...], mix[:, channels], preferred_element_type=F32)

    def swap(slot):
        return remote(xout.at[slot], xin.at[slot], xsend.at[slot], xrecv.at[slot], mate)

    def back_copy(tap):
        return remote(
            qout.at[tap - 1], rin.at[tap - 1], qsend.at[tap - 1], qrecv.at[tap - 1], (grp, tm - tap, chan)
        )

    def give(slot, part):
        def one(col):
            xout[slot, :, pl.ds(col, TILE)] = part(there, col).astype(BF16)

        tiles(one)
        swap(slot).start()

    def tap_part(tap):
        return lambda base, col: grad_part(tap, base, col)

    for tap in (2, 1):
        give(tap, tap_part(tap))
    for tap in (2, 1):
        def one(col):
            keep[:, pl.ds(col, TILE)] = grad_part(tap, here, col)

        tiles(one)
        swap(tap).wait_recv()
        qout[tap - 1] = (keep[...] + xin[tap].astype(F32)).astype(BF16)
        pl.when(tm >= tap)(lambda: back_copy(tap).start())
    give(3, mix_part)
    give(0, tap_part(0))

    def out_tile(col):
        keep[:, pl.ds(col, TILE)] = mix_part(here, col)

    tiles(out_tile)
    swap(3).wait_recv()
    out_ref[...] = (
        sig[0, :, lanes(here, half)].astype(F32) + (keep[...] + xin[3].astype(F32))
    ).astype(BF16)

    def ig_tile(col):
        keep[:, pl.ds(col, TILE)] = grad_part(0, here, col)

    tiles(ig_tile)
    swap(0).wait_recv()
    keep[...] = keep[...] + xin[0].astype(F32) + cot[:, lanes(here, half)].astype(F32)
    for tap in (1, 2):
        pl.when(tm + tap <= last)(lambda: back_copy(tap).wait_recv())
    ig_ref[...] = (keep[...] + rin[0].astype(F32) + rin[1].astype(F32)).astype(BF16)

    pl.when(has_up)(lambda: halo(0, 2, up).wait_send())
    pl.when(x == 0)(lambda: halo(0, 1, side).wait_send())
    pl.when(jnp.logical_and(x == 1, has_down))(lambda: halo(2, 1, side).wait_send())
    for lag in (1, 2):
        pl.when(tm >= lag)(lambda: to_mate(lag, here).wait_send())
        pl.when(tm >= lag)(lambda: back_copy(lag).wait_send())
    to_mate(0, here).wait_send()
    cot_copy(here).wait_send()
    for slot in range(4):
        swap(slot).wait_send()

    for step in range(DEPTH):
        ring_round(step, mix_piece, sent, skip, False)

    def drain(tap):
        for step in range(DEPTH):
            ring_round(step, w_make(tap), sent, skip, True)
            side_round(step, w_make(tap), sent, skip, True)

    each_tap(drain)


def fused_device(signal, filter_weight, gate_weight, filter_bias, gate_bias, mix_weight, cotangent):
    steps, half = signal.shape
    hid = filter_weight.shape[2]
    count = lax.axis_size("tm")
    width = count * filter_weight.shape[1]
    anywhere = pl.BlockSpec(memory_space=pl.ANY)
    vmem = pl.BlockSpec(memory_space=pltpu.VMEM)
    dma = pltpu.SemaphoreType.DMA
    return pl.pallas_call(
        fused_kernel,
        out_shape=(
            jax.ShapeDtypeStruct((steps, half), BF16),
            jax.ShapeDtypeStruct((steps, half), BF16),
        ),
        in_specs=[anywhere, anywhere, anywhere, vmem, vmem, anywhere, anywhere],
        out_specs=(vmem, vmem),
        scratch_shapes=[
            pltpu.VMEM((2, KERNEL_TAPS, width, hid), BF16),
            pltpu.VMEM((hid, width), BF16),
            pltpu.VMEM((KERNEL_TAPS, steps, width), BF16),
            pltpu.VMEM((steps, width), BF16),
            pltpu.VMEM((steps, 2 * hid), BF16),
            pltpu.VMEM((steps, hid), BF16),
            pltpu.VMEM((steps, half), F32),
            pltpu.VMEM((4, steps, half), BF16),
            pltpu.VMEM((4, steps, half), BF16),
            pltpu.VMEM((2, steps, half), BF16),
            pltpu.VMEM((2, steps, half), BF16),
            dma((4, KERNEL_TAPS, count)),
            dma((2, KERNEL_TAPS, count)),
            dma((3, count)),
            dma((count,)),
            dma((3,)),
            dma((3,)),
            dma((3,)),
            dma((3,)),
            dma((1,)),
            dma((1,)),
            dma((4,)),
            dma((4,)),
            dma((2,)),
            dma((2,)),
            dma((5,)),
        ],
        compiler_params=pltpu.CompilerParams(
            collective_id=0, has_side_effects=True, vmem_limit_bytes=56 * 1024 * 1024
        ),
    )(
        signal, filter_weight, gate_weight, filter_bias.reshape(1, -1), gate_bias.reshape(1, -1),
        mix_weight, cotangent,
    )


def solution(mesh):
    in_specs = (
        P(("grp", "tm"), "chan"),
        P(None, "tm", "chan"),
        P(None, "tm", "chan"),
        P("chan"),
        P("chan"),
        P("chan", "tm"),
        P(("grp", "tm"), "chan"),
    )
    out_specs = (P(("grp", "tm"), "chan"), P(("grp", "tm"), "chan"))
    fits = mesh.shape["tm"] == 2 * DEPTH and mesh.shape["grp"] == 2 and mesh.shape["chan"] == 2
    return jax.shard_map(
        fused_device if fits else per_device, mesh=mesh, in_specs=in_specs, out_specs=out_specs, check_vma=False
    )
```

```python
import jax
import jax.numpy as jnp
from jax import lax
from jax.experimental import pallas as pl
from jax.experimental.pallas import tpu as pltpu
from jax.sharding import PartitionSpec as P

KERNEL_TAPS = 3
DILATION_STEPS = 512


def shifted(value, axis, steps):
    count = lax.axis_size(axis)
    leading, last = (max(0, -steps), min(count, count - steps))
    return lax.ppermute(value, axis, [(source, source + steps) for source in range(leading, last)])


def fetch_before(block, receptive_rows):
    sequence_length = block.shape[0]
    hop_count = -(-receptive_rows // sequence_length)
    pieces = []
    for hop_index in range(1, hop_count + 1):
        pieces.insert(0, shifted(block, "tm", hop_index))
    joined = jnp.concatenate(pieces, axis=0)
    return joined


def fetch_after(block, receptive_rows):
    sequence_length = block.shape[0]
    hop_count = -(-receptive_rows // sequence_length)
    pieces = []
    for hop_index in range(1, hop_count + 1):
        pieces.append(shifted(block, "tm", -hop_index))
    joined = jnp.concatenate(pieces, axis=0)
    return joined


def per_device(signal, filter_weight, gate_weight, filter_bias, gate_bias, mix_weight, cotangent):
    sequence_length = signal.shape[0]
    receptive_rows = (KERNEL_TAPS - 1) * DILATION_STEPS
    filter_full, gate_full, mix_full = (
        lax.all_gather(filter_weight, "tm", axis=1, tiled=True),
        lax.all_gather(gate_weight, "tm", axis=1, tiled=True),
        lax.all_gather(mix_weight, "tm", axis=1, tiled=True),
    )
    half_hidden = filter_full.shape[2]
    stacked = jnp.concatenate([filter_full, gate_full], axis=2)
    whole = lax.all_gather(signal, "chan", axis=1, tiled=True)
    earlier = fetch_before(whole, receptive_rows)
    padded_input = jnp.concatenate([earlier, whole], axis=0)
    lagged = jnp.concatenate(
        [
            padded_input[
                receptive_rows
                - tap_position * DILATION_STEPS : receptive_rows
                - tap_position * DILATION_STEPS
                + sequence_length
            ]
            for tap_position in range(KERNEL_TAPS)
        ],
        axis=1,
    )
    bias_both = jnp.concatenate([filter_bias, gate_bias])
    pre_both = (
        jnp.dot(lagged, stacked.reshape(-1, stacked.shape[2]), preferred_element_type=jnp.float32)
        + bias_both
    )
    tangent = jnp.tanh(pre_both[:, :half_hidden])
    opened = jax.nn.sigmoid(pre_both[:, half_hidden:])
    hidden = (tangent * opened).astype(jnp.bfloat16)
    mixed = lax.psum_scatter(
        jnp.dot(hidden, mix_full, preferred_element_type=jnp.float32).astype(jnp.bfloat16),
        "chan",
        scatter_dimension=1,
        tiled=True,
    ).astype(jnp.float32)
    output = (signal.astype(jnp.float32) + mixed).astype(jnp.bfloat16)
    cot_whole = lax.all_gather(cotangent, "chan", axis=1, tiled=True)
    back_hidden = lax.dot_general(
        cot_whole, mix_full, (((1,), (1,)), ((), ())), preferred_element_type=jnp.float32
    )
    grad_filter = (back_hidden * opened * (1.0 - tangent * tangent)).astype(jnp.bfloat16)
    grad_gate = (back_hidden * tangent * opened * (1.0 - opened)).astype(jnp.bfloat16)
    grad_both = jnp.concatenate([grad_filter, grad_gate], axis=1)
    later = fetch_after(grad_both, receptive_rows)
    forward_rows = jnp.concatenate([grad_both, later], axis=0)
    total = jnp.zeros((sequence_length, stacked.shape[1]), jnp.float32)
    for tap_position in range(KERNEL_TAPS):
        input_window = forward_rows[
            tap_position * DILATION_STEPS : tap_position * DILATION_STEPS + sequence_length
        ]
        total = total + lax.dot_general(
            input_window,
            stacked[tap_position],
            (((1,), (1,)), ((), ())),
            preferred_element_type=jnp.float32,
        )
    input_part = lax.psum_scatter(
        total.astype(jnp.bfloat16), "chan", scatter_dimension=1, tiled=True
    ).astype(jnp.float32)
    input_grad = (cotangent.astype(jnp.float32) + input_part).astype(jnp.bfloat16)
    return (output, input_grad)

F32 = jnp.float32
BF16 = jnp.bfloat16
NT = (((1,), (1,)), ((), ()))
DEPTH = 4
TILE = 256


def fused_kernel(
    signal_ref, filter_ref, gate_ref, fbias_ref, gbias_ref, mixw_ref, cot_ref,
    out_ref, ig_ref,
    w, mix, sig, cot, grads, hidden, keep, xout, xin, qout, rin,
    wsend, wrecv, msend, mrecv, ssend, srecv, fsend, frecv, csend, crecv,
    xsend, xrecv, qsend, qrecv, local, pre, backs,
):
    grp, tm, chan = lax.axis_index("grp"), lax.axis_index("tm"), lax.axis_index("chan")
    z, x = tm // 2, tm % 2
    rows = filter_ref.shape[1]
    half = cot_ref.shape[1]
    last = 2 * DEPTH - 1
    circ = (grp + chan) % 2
    other = 1 - circ
    here = chan * half
    there = (1 - chan) * half

    up, down = (grp, tm + 2, chan), (grp, tm - 2, chan)
    side, twin, mate = (grp, tm + 1 - 2 * x, chan), (1 - grp, tm, chan), (grp, tm, 1 - chan)
    has_up, has_down = z < DEPTH - 1, z > 0
    corner_at = tm - 1 + 2 * x
    has_corner = jnp.logical_and(corner_at >= 0, corner_at <= last)

    def lanes(start, size):
        return pl.ds(pl.multiple_of(start, 128), size)

    def remote(src, dst, send, recv, to):
        return pltpu.make_async_remote_copy(
            src_ref=src, dst_ref=dst, send_sem=send, recv_sem=recv,
            device_id=to, device_id_type=pl.DeviceIdType.MESH,
        )

    own_copies = [
        pltpu.make_async_copy(filter_ref, w.at[0, :, lanes(tm * rows, rows), :], local.at[0]),
        pltpu.make_async_copy(gate_ref, w.at[1, :, lanes(tm * rows, rows), :], local.at[1]),
        pltpu.make_async_copy(mixw_ref, mix.at[:, lanes(tm * rows, rows)], local.at[2]),
        pltpu.make_async_copy(signal_ref, sig.at[0, :, lanes(here, half)], local.at[3]),
        pltpu.make_async_copy(cot_ref, cot.at[:, lanes(here, half)], local.at[4]),
    ]
    for copy in own_copies:
        copy.start()

    barrier = pltpu.get_barrier_semaphore()

    def greet(to):
        pl.semaphore_signal(barrier, inc=1, device_id=to, device_id_type=pl.DeviceIdType.MESH)

    greet(side)
    greet(twin)
    greet(mate)
    pl.when(has_up)(lambda: greet(up))
    pl.when(has_down)(lambda: greet(down))
    pl.when(has_corner)(lambda: greet((grp, corner_at, chan)))
    pl.semaphore_wait(
        barrier,
        3 + has_up.astype(jnp.int32) + has_down.astype(jnp.int32) + has_corner.astype(jnp.int32),
    )

    def halo(held, lag, to):
        return remote(
            sig.at[held, :, lanes(here, half)], sig.at[lag, :, lanes(here, half)],
            ssend.at[lag], srecv.at[lag], to,
        )

    def to_mate(lag, columns):
        return remote(
            sig.at[lag, :, lanes(columns, half)], sig.at[lag, :, lanes(columns, half)],
            fsend.at[lag], frecv.at[lag], mate,
        )

    def cot_copy(columns):
        return remote(
            cot.at[:, lanes(columns, half)], cot.at[:, lanes(columns, half)],
            csend.at[0], crecv.at[0], mate,
        )

    peers = (up, down, side, twin)

    def piece(array, tap, shard, way):
        slot = w.at[array, tap, lanes(shard * rows, rows), :]
        return remote(slot, slot, wsend.at[way, tap, shard], wrecv.at[array, tap, shard], peers[way])

    def mix_piece(shard, way):
        slot = mix.at[:, lanes(shard * rows, rows)]
        return remote(slot, slot, msend.at[way, shard], mrecv.at[shard], peers[way])

    def each_tap(body):
        lax.fori_loop(0, KERNEL_TAPS, lambda tap, c: (body(tap), c)[1], 0)

    def ring_round(step, make, act, arrive, hand_over):
        if step == 0:
            pl.when(has_up)(lambda: act(make(tm, 0)))
            pl.when(has_down)(lambda: act(make(tm, 1)))
            act(make(tm, 2))
            return

        @pl.when(z >= step)
        def _():
            shard = tm - 2 * step
            arrive(make(shard, 2))
            pl.when(has_up)(lambda: act(make(shard, 0)))
            act(make(shard, 2))
            if hand_over:
                act(make(shard, 3))

        @pl.when(z + step < DEPTH)
        def _():
            shard = tm + 2 * step
            arrive(make(shard, 2))
            pl.when(has_down)(lambda: act(make(shard, 1)))
            act(make(shard, 2))
            if hand_over:
                act(make(shard, 3))

    def side_round(step, make, act, arrive, hand_over):
        def one(shard):
            arrive(make(shard, 2))
            if hand_over:
                act(make(shard, 3))

        base = tm + 1 - 2 * x
        if step == 0:
            one(base)
            return
        pl.when(z >= step)(lambda: one(base - 2 * step))
        pl.when(z + step < DEPTH)(lambda: one(base + 2 * step))

    start = lambda copy: copy.start()
    sent = lambda copy: copy.wait_send()
    landed = lambda copy: copy.wait_recv()
    skip = lambda copy: None

    def w_make(tap):
        return lambda shard, way: piece(circ, tap, shard, way)

    own_copies[3].wait()
    own_copies[2].wait()
    ring_round(0, mix_piece, start, landed, False)
    own_copies[0].wait()
    own_copies[1].wait()
    each_tap(lambda tap: ring_round(0, w_make(tap), start, landed, True))
    pl.when(has_up)(lambda: halo(0, 2, up).start())
    pl.when(x == 0)(lambda: halo(0, 1, side).start())
    to_mate(0, here).start()
    own_copies[4].wait()
    cot_copy(here).start()

    for lag in (1, 2):
        @pl.when(tm < lag)
        def _():
            sig[lag] = jnp.zeros_like(sig[lag])

        @pl.when(tm + lag > last)
        def _():
            rin[lag - 1] = jnp.zeros_like(rin[lag - 1])

    for step in range(1, DEPTH):
        ring_round(step, mix_piece, start, landed, False)
        side_round(step - 1, mix_piece, start, landed, False)

        def body(tap):
            ring_round(step, w_make(tap), start, landed, True)
            side_round(step - 1, w_make(tap), start, landed, True)

        each_tap(body)
        if step == 1:
            @pl.when(has_down)
            def _():
                halo(0, 2, side).wait_recv()
                pl.when(x == 1)(lambda: halo(2, 1, side).start())
                to_mate(2, here).start()

        if step == 2:
            @pl.when(tm >= 1)
            def _():
                halo(0, 1, side).wait_recv()
                to_mate(1, here).start()
    side_round(DEPTH - 1, mix_piece, start, landed, False)
    each_tap(lambda tap: side_round(DEPTH - 1, w_make(tap), start, landed, True))

    to_mate(0, there).wait_recv()
    for lag in (1, 2):
        pl.when(tm >= lag)(lambda: to_mate(lag, there).wait_recv())
    cot_copy(there).wait_recv()

    def other_landed(tap):
        def one(step, c):
            piece(other, tap, (tm + step) % (last + 1), 3).wait_recv()
            return c

        lax.fori_loop(1, last + 1, one, 0)

    def tiles(body):
        def one(i, c):
            body(pl.multiple_of(i * TILE, TILE))
            return c

        lax.fori_loop(0, half // TILE, one, 0)

    def early(col):
        columns = pl.ds(col, TILE)
        total = jnp.dot(sig[0], w[circ, 0, :, columns], preferred_element_type=F32)
        for tap in range(1, KERNEL_TAPS):
            total += jnp.dot(sig[tap], w[circ, tap, :, columns], preferred_element_type=F32)
        pre[circ, :, columns] = total
        backs[:, columns] = lax.dot_general(cot[...], mix[columns, :], NT, preferred_element_type=F32)

    tiles(early)

    for tap in range(KERNEL_TAPS):
        other_landed(tap)

        def late(col):
            columns = pl.ds(col, TILE)
            part = jnp.dot(sig[tap], w[other, tap, :, columns], preferred_element_type=F32)
            pre[other, :, columns] = part if tap == 0 else pre[other, :, columns] + part

        tiles(late)

    def forward(col):
        columns = pl.ds(col, TILE)
        pre_f = pre[0, :, columns] + fbias_ref[:, columns]
        pre_g = pre[1, :, columns] + gbias_ref[:, columns]
        t = jnp.tanh(pre_f)
        s = jax.nn.sigmoid(pre_g)
        ts = t * s
        hidden[:, columns] = ts.astype(BF16)
        back = backs[:, columns]
        grads[:, columns] = (back * s * (1.0 - t * t)).astype(BF16)
        grads[:, pl.ds(pl.multiple_of(half + col, TILE), TILE)] = (back * ts * (1.0 - s)).astype(BF16)

    tiles(forward)

    def grad_part(tap, base, col):
        channels = pl.ds(pl.multiple_of(base + col, TILE), TILE)
        return lax.dot_general(
            grads[:, :half], w[0, tap, channels, :], NT, preferred_element_type=F32
        ) + lax.dot_general(grads[:, half:], w[1, tap, channels, :], NT, preferred_element_type=F32)

    def mix_part(base, col):
        channels = pl.ds(pl.multiple_of(base + col, TILE), TILE)
        return jnp.dot(hidden[...], mix[:, channels], preferred_element_type=F32)

    def swap(slot):
        return remote(xout.at[slot], xin.at[slot], xsend.at[slot], xrecv.at[slot], mate)

    def back_copy(tap):
        return remote(
            qout.at[tap - 1], rin.at[tap - 1], qsend.at[tap - 1], qrecv.at[tap - 1], (grp, tm - tap, chan)
        )

    def give(slot, part):
        def one(col):
            xout[slot, :, pl.ds(col, TILE)] = part(there, col).astype(BF16)

        tiles(one)
        swap(slot).start()

    def tap_part(tap):
        return lambda base, col: grad_part(tap, base, col)

    for tap in (2, 1):
        give(tap, tap_part(tap))
    for tap in (2, 1):
        def one(col):
            keep[:, pl.ds(col, TILE)] = grad_part(tap, here, col)

        tiles(one)
        swap(tap).wait_recv()
        qout[tap - 1] = (keep[...] + xin[tap].astype(F32)).astype(BF16)
        pl.when(tm >= tap)(lambda: back_copy(tap).start())
    give(3, mix_part)
    give(0, tap_part(0))

    def out_tile(col):
        keep[:, pl.ds(col, TILE)] = mix_part(here, col)

    tiles(out_tile)
    swap(3).wait_recv()
    out_ref[...] = (
        sig[0, :, lanes(here, half)].astype(F32) + (keep[...] + xin[3].astype(F32))
    ).astype(BF16)

    def ig_tile(col):
        keep[:, pl.ds(col, TILE)] = grad_part(0, here, col)

    tiles(ig_tile)
    swap(0).wait_recv()
    keep[...] = keep[...] + xin[0].astype(F32) + cot[:, lanes(here, half)].astype(F32)
    for tap in (1, 2):
        pl.when(tm + tap <= last)(lambda: back_copy(tap).wait_recv())
    ig_ref[...] = (keep[...] + rin[0].astype(F32) + rin[1].astype(F32)).astype(BF16)

    pl.when(has_up)(lambda: halo(0, 2, up).wait_send())
    pl.when(x == 0)(lambda: halo(0, 1, side).wait_send())
    pl.when(jnp.logical_and(x == 1, has_down))(lambda: halo(2, 1, side).wait_send())
    for lag in (1, 2):
        pl.when(tm >= lag)(lambda: to_mate(lag, here).wait_send())
        pl.when(tm >= lag)(lambda: back_copy(lag).wait_send())
    to_mate(0, here).wait_send()
    cot_copy(here).wait_send()
    for slot in range(4):
        swap(slot).wait_send()

    for step in range(DEPTH):
        ring_round(step, mix_piece, sent, skip, False)

    def drain(tap):
        for step in range(DEPTH):
            ring_round(step, w_make(tap), sent, skip, True)
            side_round(step, w_make(tap), sent, skip, True)

    each_tap(drain)


def fused_device(signal, filter_weight, gate_weight, filter_bias, gate_bias, mix_weight, cotangent):
    steps, half = signal.shape
    hid = filter_weight.shape[2]
    count = lax.axis_size("tm")
    width = count * filter_weight.shape[1]
    anywhere = pl.BlockSpec(memory_space=pl.ANY)
    vmem = pl.BlockSpec(memory_space=pltpu.VMEM)
    dma = pltpu.SemaphoreType.DMA
    return pl.pallas_call(
        fused_kernel,
        out_shape=(
            jax.ShapeDtypeStruct((steps, half), BF16),
            jax.ShapeDtypeStruct((steps, half), BF16),
        ),
        in_specs=[anywhere, anywhere, anywhere, vmem, vmem, anywhere, anywhere],
        out_specs=(vmem, vmem),
        scratch_shapes=[
            pltpu.VMEM((2, KERNEL_TAPS, width, hid), BF16),
            pltpu.VMEM((hid, width), BF16),
            pltpu.VMEM((KERNEL_TAPS, steps, width), BF16),
            pltpu.VMEM((steps, width), BF16),
            pltpu.VMEM((steps, 2 * hid), BF16),
            pltpu.VMEM((steps, hid), BF16),
            pltpu.VMEM((steps, half), F32),
            pltpu.VMEM((4, steps, half), BF16),
            pltpu.VMEM((4, steps, half), BF16),
            pltpu.VMEM((2, steps, half), BF16),
            pltpu.VMEM((2, steps, half), BF16),
            dma((4, KERNEL_TAPS, count)),
            dma((2, KERNEL_TAPS, count)),
            dma((3, count)),
            dma((count,)),
            dma((3,)),
            dma((3,)),
            dma((3,)),
            dma((3,)),
            dma((1,)),
            dma((1,)),
            dma((4,)),
            dma((4,)),
            dma((2,)),
            dma((2,)),
            dma((5,)),
            pltpu.VMEM((2, steps, hid), F32),
            pltpu.VMEM((steps, hid), F32),
        ],
        compiler_params=pltpu.CompilerParams(
            collective_id=0, has_side_effects=True, vmem_limit_bytes=56 * 1024 * 1024
        ),
    )(
        signal, filter_weight, gate_weight, filter_bias.reshape(1, -1), gate_bias.reshape(1, -1),
        mix_weight, cotangent,
    )


def solution(mesh):
    in_specs = (
        P(("grp", "tm"), "chan"),
        P(None, "tm", "chan"),
        P(None, "tm", "chan"),
        P("chan"),
        P("chan"),
        P("chan", "tm"),
        P(("grp", "tm"), "chan"),
    )
    out_specs = (P(("grp", "tm"), "chan"), P(("grp", "tm"), "chan"))
    fits = mesh.shape["tm"] == 2 * DEPTH and mesh.shape["grp"] == 2 and mesh.shape["chan"] == 2
    return jax.shard_map(
        fused_device if fits else per_device, mesh=mesh, in_specs=in_specs, out_specs=out_specs, check_vma=False
    )
```

```python
import jax
import jax.numpy as jnp
from jax import lax
from jax.experimental import pallas as pl
from jax.experimental.pallas import tpu as pltpu
from jax.sharding import PartitionSpec as P

KERNEL_TAPS = 3
DILATION_STEPS = 512


def shifted(value, axis, steps):
    count = lax.axis_size(axis)
    leading, last = (max(0, -steps), min(count, count - steps))
    return lax.ppermute(value, axis, [(source, source + steps) for source in range(leading, last)])


def fetch_before(block, receptive_rows):
    sequence_length = block.shape[0]
    hop_count = -(-receptive_rows // sequence_length)
    pieces = []
    for hop_index in range(1, hop_count + 1):
        pieces.insert(0, shifted(block, "tm", hop_index))
    joined = jnp.concatenate(pieces, axis=0)
    return joined


def fetch_after(block, receptive_rows):
    sequence_length = block.shape[0]
    hop_count = -(-receptive_rows // sequence_length)
    pieces = []
    for hop_index in range(1, hop_count + 1):
        pieces.append(shifted(block, "tm", -hop_index))
    joined = jnp.concatenate(pieces, axis=0)
    return joined


def per_device(signal, filter_weight, gate_weight, filter_bias, gate_bias, mix_weight, cotangent):
    sequence_length = signal.shape[0]
    receptive_rows = (KERNEL_TAPS - 1) * DILATION_STEPS
    filter_full, gate_full, mix_full = (
        lax.all_gather(filter_weight, "tm", axis=1, tiled=True),
        lax.all_gather(gate_weight, "tm", axis=1, tiled=True),
        lax.all_gather(mix_weight, "tm", axis=1, tiled=True),
    )
    half_hidden = filter_full.shape[2]
    stacked = jnp.concatenate([filter_full, gate_full], axis=2)
    whole = lax.all_gather(signal, "chan", axis=1, tiled=True)
    earlier = fetch_before(whole, receptive_rows)
    padded_input = jnp.concatenate([earlier, whole], axis=0)
    lagged = jnp.concatenate(
        [
            padded_input[
                receptive_rows
                - tap_position * DILATION_STEPS : receptive_rows
                - tap_position * DILATION_STEPS
                + sequence_length
            ]
            for tap_position in range(KERNEL_TAPS)
        ],
        axis=1,
    )
    bias_both = jnp.concatenate([filter_bias, gate_bias])
    pre_both = (
        jnp.dot(lagged, stacked.reshape(-1, stacked.shape[2]), preferred_element_type=jnp.float32)
        + bias_both
    )
    tangent = jnp.tanh(pre_both[:, :half_hidden])
    opened = jax.nn.sigmoid(pre_both[:, half_hidden:])
    hidden = (tangent * opened).astype(jnp.bfloat16)
    mixed = lax.psum_scatter(
        jnp.dot(hidden, mix_full, preferred_element_type=jnp.float32).astype(jnp.bfloat16),
        "chan",
        scatter_dimension=1,
        tiled=True,
    ).astype(jnp.float32)
    output = (signal.astype(jnp.float32) + mixed).astype(jnp.bfloat16)
    cot_whole = lax.all_gather(cotangent, "chan", axis=1, tiled=True)
    back_hidden = lax.dot_general(
        cot_whole, mix_full, (((1,), (1,)), ((), ())), preferred_element_type=jnp.float32
    )
    grad_filter = (back_hidden * opened * (1.0 - tangent * tangent)).astype(jnp.bfloat16)
    grad_gate = (back_hidden * tangent * opened * (1.0 - opened)).astype(jnp.bfloat16)
    grad_both = jnp.concatenate([grad_filter, grad_gate], axis=1)
    later = fetch_after(grad_both, receptive_rows)
    forward_rows = jnp.concatenate([grad_both, later], axis=0)
    total = jnp.zeros((sequence_length, stacked.shape[1]), jnp.float32)
    for tap_position in range(KERNEL_TAPS):
        input_window = forward_rows[
            tap_position * DILATION_STEPS : tap_position * DILATION_STEPS + sequence_length
        ]
        total = total + lax.dot_general(
            input_window,
            stacked[tap_position],
            (((1,), (1,)), ((), ())),
            preferred_element_type=jnp.float32,
        )
    input_part = lax.psum_scatter(
        total.astype(jnp.bfloat16), "chan", scatter_dimension=1, tiled=True
    ).astype(jnp.float32)
    input_grad = (cotangent.astype(jnp.float32) + input_part).astype(jnp.bfloat16)
    return (output, input_grad)

F32 = jnp.float32
BF16 = jnp.bfloat16
NT = (((1,), (1,)), ((), ()))
DEPTH = 4
TILE = 256
CHUNKS = 4


def fused_kernel(
    signal_ref, filter_ref, gate_ref, fbias_ref, gbias_ref, mixw_ref, cot_ref,
    out_ref, ig_ref,
    w, mix, sig, cot, grads, hidden, keep, xout, xin, qout, rin,
    wsend, wrecv, msend, mrecv, ssend, srecv, fsend, frecv, csend, crecv,
    xsend, xrecv, qsend, qrecv, local, pre, backs,
):
    grp, tm, chan = lax.axis_index("grp"), lax.axis_index("tm"), lax.axis_index("chan")
    z, x = tm // 2, tm % 2
    rows = filter_ref.shape[1]
    half = cot_ref.shape[1]
    last = 2 * DEPTH - 1
    circ = (grp + chan) % 2
    other = 1 - circ
    here = chan * half
    there = (1 - chan) * half

    up, down = (grp, tm + 2, chan), (grp, tm - 2, chan)
    side, twin, mate = (grp, tm + 1 - 2 * x, chan), (1 - grp, tm, chan), (grp, tm, 1 - chan)
    has_up, has_down = z < DEPTH - 1, z > 0

    def lanes(start, size):
        return pl.ds(pl.multiple_of(start, 128), size)

    def remote(src, dst, send, recv, to):
        return pltpu.make_async_remote_copy(
            src_ref=src, dst_ref=dst, send_sem=send, recv_sem=recv,
            device_id=to, device_id_type=pl.DeviceIdType.MESH,
        )

    own_copies = [
        pltpu.make_async_copy(filter_ref, w.at[0, :, lanes(tm * rows, rows), :], local.at[0]),
        pltpu.make_async_copy(gate_ref, w.at[1, :, lanes(tm * rows, rows), :], local.at[1]),
        pltpu.make_async_copy(mixw_ref, mix.at[:, lanes(tm * rows, rows)], local.at[2]),
        pltpu.make_async_copy(signal_ref, sig.at[0, :, lanes(here, half)], local.at[3]),
        pltpu.make_async_copy(cot_ref, cot.at[:, lanes(here, half)], local.at[4]),
    ]
    for copy in own_copies:
        copy.start()

    barrier = pltpu.get_barrier_semaphore()

    def greet(to):
        pl.semaphore_signal(barrier, inc=1, device_id=to, device_id_type=pl.DeviceIdType.MESH)

    greet(side)
    greet(twin)
    greet(mate)
    pl.when(has_up)(lambda: greet(up))
    pl.when(has_down)(lambda: greet(down))
    pl.semaphore_wait(barrier, 3 + has_up.astype(jnp.int32) + has_down.astype(jnp.int32))

    def halo(held, lag, to):
        return remote(
            sig.at[held, :, lanes(here, half)], sig.at[lag, :, lanes(here, half)],
            ssend.at[lag], srecv.at[lag], to,
        )

    def to_mate(lag, columns):
        return remote(
            sig.at[lag, :, lanes(columns, half)], sig.at[lag, :, lanes(columns, half)],
            fsend.at[lag], frecv.at[lag], mate,
        )

    def cot_copy(columns):
        return remote(
            cot.at[:, lanes(columns, half)], cot.at[:, lanes(columns, half)],
            csend.at[0], crecv.at[0], mate,
        )

    peers = (up, down, side, twin)

    def piece(array, tap, shard, way):
        slot = w.at[array, tap, lanes(shard * rows, rows), :]
        return remote(slot, slot, wsend.at[way, tap, shard], wrecv.at[array, tap, shard], peers[way])

    def mix_piece(shard, way):
        slot = mix.at[:, lanes(shard * rows, rows)]
        return remote(slot, slot, msend.at[way, shard], mrecv.at[shard], peers[way])

    def each_tap(body):
        lax.fori_loop(0, KERNEL_TAPS, lambda tap, c: (body(tap), c)[1], 0)

    def ring_round(step, make, act, arrive, hand_over):
        if step == 0:
            pl.when(has_up)(lambda: act(make(tm, 0)))
            pl.when(has_down)(lambda: act(make(tm, 1)))
            act(make(tm, 2))
            return

        @pl.when(z >= step)
        def _():
            shard = tm - 2 * step
            arrive(make(shard, 2))
            pl.when(has_up)(lambda: act(make(shard, 0)))
            act(make(shard, 2))
            if hand_over:
                act(make(shard, 3))

        @pl.when(z + step < DEPTH)
        def _():
            shard = tm + 2 * step
            arrive(make(shard, 2))
            pl.when(has_down)(lambda: act(make(shard, 1)))
            act(make(shard, 2))
            if hand_over:
                act(make(shard, 3))

    def side_round(step, make, act, arrive, hand_over):
        def one(shard):
            arrive(make(shard, 2))
            if hand_over:
                act(make(shard, 3))

        base = tm + 1 - 2 * x
        if step == 0:
            one(base)
            return
        pl.when(z >= step)(lambda: one(base - 2 * step))
        pl.when(z + step < DEPTH)(lambda: one(base + 2 * step))

    start = lambda copy: copy.start()
    sent = lambda copy: copy.wait_send()
    landed = lambda copy: copy.wait_recv()
    skip = lambda copy: None

    def w_make(tap):
        return lambda shard, way: piece(circ, tap, shard, way)

    own_copies[3].wait()
    own_copies[2].wait()
    ring_round(0, mix_piece, start, landed, False)
    own_copies[0].wait()
    own_copies[1].wait()
    each_tap(lambda tap: ring_round(0, w_make(tap), start, landed, True))
    pl.when(has_up)(lambda: halo(0, 2, up).start())
    pl.when(x == 0)(lambda: halo(0, 1, side).start())
    to_mate(0, here).start()
    own_copies[4].wait()
    cot_copy(here).start()

    for lag in (1, 2):
        @pl.when(tm < lag)
        def _():
            sig[lag] = jnp.zeros_like(sig[lag])

    @pl.when(jnp.logical_not(has_up))
    def _():
        rin[1] = jnp.zeros_like(rin[1])

    for step in range(1, DEPTH):
        def body(tap):
            ring_round(step, w_make(tap), start, landed, True)
            side_round(step - 1, w_make(tap), start, landed, True)

        each_tap(body)
        ring_round(step, mix_piece, start, landed, False)
        side_round(step - 1, mix_piece, start, landed, False)
        if step == 1:
            @pl.when(has_down)
            def _():
                halo(0, 2, side).wait_recv()
                pl.when(x == 1)(lambda: halo(2, 1, side).start())
                to_mate(2, here).start()

        if step == 2:
            @pl.when(tm >= 1)
            def _():
                halo(0, 1, side).wait_recv()
                to_mate(1, here).start()
    side_round(DEPTH - 1, mix_piece, start, landed, False)
    each_tap(lambda tap: side_round(DEPTH - 1, w_make(tap), start, landed, True))

    to_mate(0, there).wait_recv()
    for lag in (1, 2):
        pl.when(tm >= lag)(lambda: to_mate(lag, there).wait_recv())
    cot_copy(there).wait_recv()

    def other_landed(tap):
        def one(step, c):
            piece(other, tap, (tm + step) % (last + 1), 3).wait_recv()
            return c

        lax.fori_loop(1, last + 1, one, 0)

    def tiles(body):
        def one(i, c):
            body(pl.multiple_of(i * TILE, TILE))
            return c

        lax.fori_loop(0, half // TILE, one, 0)

    def early(col):
        columns = pl.ds(col, TILE)
        total = jnp.dot(sig[0], w[circ, 0, :, columns], preferred_element_type=F32)
        for tap in range(1, KERNEL_TAPS):
            total += jnp.dot(sig[tap], w[circ, tap, :, columns], preferred_element_type=F32)
        pre[circ, :, columns] = total
        backs[:, columns] = lax.dot_general(cot[...], mix[columns, :], NT, preferred_element_type=F32)

    tiles(early)

    for tap in range(KERNEL_TAPS):
        other_landed(tap)

        def late(col):
            columns = pl.ds(col, TILE)
            part = jnp.dot(sig[tap], w[other, tap, :, columns], preferred_element_type=F32)
            pre[other, :, columns] = part if tap == 0 else pre[other, :, columns] + part

        tiles(late)

    def forward(col):
        columns = pl.ds(col, TILE)
        pre_f = pre[0, :, columns] + fbias_ref[:, columns]
        pre_g = pre[1, :, columns] + gbias_ref[:, columns]
        t = jnp.tanh(pre_f)
        s = jax.nn.sigmoid(pre_g)
        ts = t * s
        hidden[:, columns] = ts.astype(BF16)
        back = backs[:, columns]
        grads[:, columns] = (back * s * (1.0 - t * t)).astype(BF16)
        grads[:, pl.ds(pl.multiple_of(half + col, TILE), TILE)] = (back * ts * (1.0 - s)).astype(BF16)

    tiles(forward)

    def grad_part(tap, base, col):
        channels = pl.ds(pl.multiple_of(base + col, TILE), TILE)
        return lax.dot_general(
            grads[:, :half], w[0, tap, channels, :], NT, preferred_element_type=F32
        ) + lax.dot_general(grads[:, half:], w[1, tap, channels, :], NT, preferred_element_type=F32)

    def mix_part(base, col):
        channels = pl.ds(pl.multiple_of(base + col, TILE), TILE)
        return jnp.dot(hidden[...], mix[:, channels], preferred_element_type=F32)

    def swap(slot):
        return remote(xout.at[slot], xin.at[slot], xsend.at[slot], xrecv.at[slot], mate)

    chunk = rin.shape[1] // CHUNKS

    def back_copy(tap, part):
        piece_rows = pl.ds(part * chunk, chunk)
        return remote(
            qout.at[tap - 1, piece_rows], rin.at[tap - 1, piece_rows],
            qsend.at[tap - 1, part], qrecv.at[tap - 1, part], side if tap == 1 else down,
        )

    def all_parts(tap, act):
        for part in range(CHUNKS):
            act(back_copy(tap, part))

    side_gives = jnp.logical_or(x == 1, has_down)
    merges = jnp.logical_and(x == 1, has_down)

    def give(slot, part):
        def one(col):
            xout[slot, :, pl.ds(col, TILE)] = part(there, col).astype(BF16)

        tiles(one)
        swap(slot).start()

    def tap_part(tap):
        return lambda base, col: grad_part(tap, base, col)

    for tap in (1, 2):
        give(tap, tap_part(tap))
    for tap in (1, 2):
        def one(col):
            keep[:, pl.ds(col, TILE)] = grad_part(tap, here, col)

        tiles(one)
        swap(tap).wait_recv()
        if tap == 1:
            qout[0] = (keep[...] + xin[1].astype(F32)).astype(BF16)
            pl.when(side_gives)(lambda: all_parts(1, start))

    keep[...] = keep[...] + xin[2].astype(F32)

    @pl.when(jnp.logical_and(x == 0, has_down))
    def _():
        qout[1] = keep[...].astype(BF16)
        all_parts(2, start)

    give(3, mix_part)
    give(0, tap_part(0))

    @pl.when(merges)
    def _():
        for part in range(CHUNKS):
            back_copy(1, part).wait_recv()
            piece_rows = pl.ds(part * chunk, chunk)
            qout[1, piece_rows] = (keep[piece_rows] + rin[0, piece_rows].astype(F32)).astype(BF16)
            back_copy(2, part).start()

    def out_tile(col):
        keep[:, pl.ds(col, TILE)] = mix_part(here, col)

    tiles(out_tile)
    swap(3).wait_recv()
    out_ref[...] = (
        sig[0, :, lanes(here, half)].astype(F32) + (keep[...] + xin[3].astype(F32))
    ).astype(BF16)

    def ig_tile(col):
        keep[:, pl.ds(col, TILE)] = grad_part(0, here, col)

    tiles(ig_tile)
    swap(0).wait_recv()
    keep[...] = keep[...] + xin[0].astype(F32) + cot[:, lanes(here, half)].astype(F32)

    @pl.when(x == 0)
    def _():
        all_parts(1, landed)
        keep[...] = keep[...] + rin[0].astype(F32)

    pl.when(has_up)(lambda: all_parts(2, landed))
    ig_ref[...] = (keep[...] + rin[1].astype(F32)).astype(BF16)

    pl.when(has_up)(lambda: halo(0, 2, up).wait_send())
    pl.when(x == 0)(lambda: halo(0, 1, side).wait_send())
    pl.when(jnp.logical_and(x == 1, has_down))(lambda: halo(2, 1, side).wait_send())
    for lag in (1, 2):
        pl.when(tm >= lag)(lambda: to_mate(lag, here).wait_send())
    to_mate(0, here).wait_send()
    cot_copy(here).wait_send()
    for slot in range(4):
        swap(slot).wait_send()
    pl.when(side_gives)(lambda: all_parts(1, sent))
    pl.when(has_down)(lambda: all_parts(2, sent))

    for step in range(DEPTH):
        ring_round(step, mix_piece, sent, skip, False)

    def drain(tap):
        for step in range(DEPTH):
            ring_round(step, w_make(tap), sent, skip, True)
            side_round(step, w_make(tap), sent, skip, True)

    each_tap(drain)


def fused_device(signal, filter_weight, gate_weight, filter_bias, gate_bias, mix_weight, cotangent):
    steps, half = signal.shape
    hid = filter_weight.shape[2]
    count = lax.axis_size("tm")
    width = count * filter_weight.shape[1]
    anywhere = pl.BlockSpec(memory_space=pl.ANY)
    vmem = pl.BlockSpec(memory_space=pltpu.VMEM)
    dma = pltpu.SemaphoreType.DMA
    return pl.pallas_call(
        fused_kernel,
        out_shape=(
            jax.ShapeDtypeStruct((steps, half), BF16),
            jax.ShapeDtypeStruct((steps, half), BF16),
        ),
        in_specs=[anywhere, anywhere, anywhere, vmem, vmem, anywhere, anywhere],
        out_specs=(vmem, vmem),
        scratch_shapes=[
            pltpu.VMEM((2, KERNEL_TAPS, width, hid), BF16),
            pltpu.VMEM((hid, width), BF16),
            pltpu.VMEM((KERNEL_TAPS, steps, width), BF16),
            pltpu.VMEM((steps, width), BF16),
            pltpu.VMEM((steps, 2 * hid), BF16),
            pltpu.VMEM((steps, hid), BF16),
            pltpu.VMEM((steps, half), F32),
            pltpu.VMEM((4, steps, half), BF16),
            pltpu.VMEM((4, steps, half), BF16),
            pltpu.VMEM((2, steps, half), BF16),
            pltpu.VMEM((2, steps, half), BF16),
            dma((4, KERNEL_TAPS, count)),
            dma((2, KERNEL_TAPS, count)),
            dma((3, count)),
            dma((count,)),
            dma((3,)),
            dma((3,)),
            dma((3,)),
            dma((3,)),
            dma((1,)),
            dma((1,)),
            dma((4,)),
            dma((4,)),
            dma((2, CHUNKS)),
            dma((2, CHUNKS)),
            dma((5,)),
            pltpu.VMEM((2, steps, hid), F32),
            pltpu.VMEM((steps, hid), F32),
        ],
        compiler_params=pltpu.CompilerParams(
            collective_id=0, has_side_effects=True, vmem_limit_bytes=56 * 1024 * 1024
        ),
    )(
        signal, filter_weight, gate_weight, filter_bias.reshape(1, -1), gate_bias.reshape(1, -1),
        mix_weight, cotangent,
    )


def solution(mesh):
    in_specs = (
        P(("grp", "tm"), "chan"),
        P(None, "tm", "chan"),
        P(None, "tm", "chan"),
        P("chan"),
        P("chan"),
        P("chan", "tm"),
        P(("grp", "tm"), "chan"),
    )
    out_specs = (P(("grp", "tm"), "chan"), P(("grp", "tm"), "chan"))
    fits = mesh.shape["tm"] == 2 * DEPTH and mesh.shape["grp"] == 2 and mesh.shape["chan"] == 2
    return jax.shard_map(
        fused_device if fits else per_device, mesh=mesh, in_specs=in_specs, out_specs=out_specs, check_vma=False
    )
```

```python
import jax
import jax.numpy as jnp
from jax import lax
from jax.experimental import pallas as pl
from jax.experimental.pallas import tpu as pltpu
from jax.sharding import PartitionSpec as P

KERNEL_TAPS = 3
DILATION_STEPS = 512


def shifted(value, axis, steps):
    count = lax.axis_size(axis)
    leading, last = (max(0, -steps), min(count, count - steps))
    return lax.ppermute(value, axis, [(source, source + steps) for source in range(leading, last)])


def fetch_before(block, receptive_rows):
    sequence_length = block.shape[0]
    hop_count = -(-receptive_rows // sequence_length)
    pieces = []
    for hop_index in range(1, hop_count + 1):
        pieces.insert(0, shifted(block, "tm", hop_index))
    joined = jnp.concatenate(pieces, axis=0)
    return joined


def fetch_after(block, receptive_rows):
    sequence_length = block.shape[0]
    hop_count = -(-receptive_rows // sequence_length)
    pieces = []
    for hop_index in range(1, hop_count + 1):
        pieces.append(shifted(block, "tm", -hop_index))
    joined = jnp.concatenate(pieces, axis=0)
    return joined


def per_device(signal, filter_weight, gate_weight, filter_bias, gate_bias, mix_weight, cotangent):
    sequence_length = signal.shape[0]
    receptive_rows = (KERNEL_TAPS - 1) * DILATION_STEPS
    filter_full, gate_full, mix_full = (
        lax.all_gather(filter_weight, "tm", axis=1, tiled=True),
        lax.all_gather(gate_weight, "tm", axis=1, tiled=True),
        lax.all_gather(mix_weight, "tm", axis=1, tiled=True),
    )
    half_hidden = filter_full.shape[2]
    stacked = jnp.concatenate([filter_full, gate_full], axis=2)
    whole = lax.all_gather(signal, "chan", axis=1, tiled=True)
    earlier = fetch_before(whole, receptive_rows)
    padded_input = jnp.concatenate([earlier, whole], axis=0)
    lagged = jnp.concatenate(
        [
            padded_input[
                receptive_rows
                - tap_position * DILATION_STEPS : receptive_rows
                - tap_position * DILATION_STEPS
                + sequence_length
            ]
            for tap_position in range(KERNEL_TAPS)
        ],
        axis=1,
    )
    bias_both = jnp.concatenate([filter_bias, gate_bias])
    pre_both = (
        jnp.dot(lagged, stacked.reshape(-1, stacked.shape[2]), preferred_element_type=jnp.float32)
        + bias_both
    )
    tangent = jnp.tanh(pre_both[:, :half_hidden])
    opened = jax.nn.sigmoid(pre_both[:, half_hidden:])
    hidden = (tangent * opened).astype(jnp.bfloat16)
    mixed = lax.psum_scatter(
        jnp.dot(hidden, mix_full, preferred_element_type=jnp.float32).astype(jnp.bfloat16),
        "chan",
        scatter_dimension=1,
        tiled=True,
    ).astype(jnp.float32)
    output = (signal.astype(jnp.float32) + mixed).astype(jnp.bfloat16)
    cot_whole = lax.all_gather(cotangent, "chan", axis=1, tiled=True)
    back_hidden = lax.dot_general(
        cot_whole, mix_full, (((1,), (1,)), ((), ())), preferred_element_type=jnp.float32
    )
    grad_filter = (back_hidden * opened * (1.0 - tangent * tangent)).astype(jnp.bfloat16)
    grad_gate = (back_hidden * tangent * opened * (1.0 - opened)).astype(jnp.bfloat16)
    grad_both = jnp.concatenate([grad_filter, grad_gate], axis=1)
    later = fetch_after(grad_both, receptive_rows)
    forward_rows = jnp.concatenate([grad_both, later], axis=0)
    total = jnp.zeros((sequence_length, stacked.shape[1]), jnp.float32)
    for tap_position in range(KERNEL_TAPS):
        input_window = forward_rows[
            tap_position * DILATION_STEPS : tap_position * DILATION_STEPS + sequence_length
        ]
        total = total + lax.dot_general(
            input_window,
            stacked[tap_position],
            (((1,), (1,)), ((), ())),
            preferred_element_type=jnp.float32,
        )
    input_part = lax.psum_scatter(
        total.astype(jnp.bfloat16), "chan", scatter_dimension=1, tiled=True
    ).astype(jnp.float32)
    input_grad = (cotangent.astype(jnp.float32) + input_part).astype(jnp.bfloat16)
    return (output, input_grad)

F32 = jnp.float32
BF16 = jnp.bfloat16
NT = (((1,), (1,)), ((), ()))
DEPTH = 4
TILE = 256
CHUNKS = 8


def fused_kernel(
    signal_ref, filter_ref, gate_ref, fbias_ref, gbias_ref, mixw_ref, cot_ref,
    out_ref, ig_ref,
    w, mix, sig, cot, grads, hidden, keep, xout, xin, qout, rin,
    wsend, wrecv, msend, mrecv, ssend, srecv, fsend, frecv, csend, crecv,
    xsend, xrecv, qsend, qrecv, local, pre, backs, mix_parts,
):
    grp, tm, chan = lax.axis_index("grp"), lax.axis_index("tm"), lax.axis_index("chan")
    z, x = tm // 2, tm % 2
    rows = filter_ref.shape[1]
    half = cot_ref.shape[1]
    last = 2 * DEPTH - 1
    circ = (grp + chan) % 2
    other = 1 - circ
    here = chan * half
    there = (1 - chan) * half

    up, down = (grp, tm + 2, chan), (grp, tm - 2, chan)
    side, twin, mate = (grp, tm + 1 - 2 * x, chan), (1 - grp, tm, chan), (grp, tm, 1 - chan)
    has_up, has_down = z < DEPTH - 1, z > 0

    def lanes(start, size):
        return pl.ds(pl.multiple_of(start, 128), size)

    def remote(src, dst, send, recv, to):
        return pltpu.make_async_remote_copy(
            src_ref=src, dst_ref=dst, send_sem=send, recv_sem=recv,
            device_id=to, device_id_type=pl.DeviceIdType.MESH,
        )

    own_copies = [
        pltpu.make_async_copy(filter_ref, w.at[0, :, lanes(tm * rows, rows), :], local.at[0]),
        pltpu.make_async_copy(gate_ref, w.at[1, :, lanes(tm * rows, rows), :], local.at[1]),
        pltpu.make_async_copy(mixw_ref, mix_parts.at[tm], local.at[2]),
        pltpu.make_async_copy(signal_ref, sig.at[0, :, lanes(here, half)], local.at[3]),
        pltpu.make_async_copy(cot_ref, cot.at[:, lanes(here, half)], local.at[4]),
    ]
    for copy in own_copies:
        copy.start()

    barrier = pltpu.get_barrier_semaphore()

    def greet(to):
        pl.semaphore_signal(barrier, inc=1, device_id=to, device_id_type=pl.DeviceIdType.MESH)

    greet(side)
    greet(twin)
    greet(mate)
    pl.when(has_up)(lambda: greet(up))
    pl.when(has_down)(lambda: greet(down))
    pl.semaphore_wait(barrier, 3 + has_up.astype(jnp.int32) + has_down.astype(jnp.int32))

    def halo(held, lag, to):
        return remote(
            sig.at[held, :, lanes(here, half)], sig.at[lag, :, lanes(here, half)],
            ssend.at[lag], srecv.at[lag], to,
        )

    def to_mate(lag, columns):
        return remote(
            sig.at[lag, :, lanes(columns, half)], sig.at[lag, :, lanes(columns, half)],
            fsend.at[lag], frecv.at[lag], mate,
        )

    def cot_copy(columns):
        return remote(
            cot.at[:, lanes(columns, half)], cot.at[:, lanes(columns, half)],
            csend.at[0], crecv.at[0], mate,
        )

    peers = (up, down, side, twin)

    def piece(array, tap, shard, way):
        slot = w.at[array, tap, lanes(shard * rows, rows), :]
        return remote(slot, slot, wsend.at[way, tap, shard], wrecv.at[array, tap, shard], peers[way])

    def mix_piece(shard, way):
        slot = mix_parts.at[shard]
        return remote(slot, slot, msend.at[way, shard], mrecv.at[shard], peers[way])

    def each_tap(body):
        lax.fori_loop(0, KERNEL_TAPS, lambda tap, c: (body(tap), c)[1], 0)

    def ring_round(step, make, act, arrive, hand_over):
        if step == 0:
            pl.when(has_up)(lambda: act(make(tm, 0)))
            pl.when(has_down)(lambda: act(make(tm, 1)))
            act(make(tm, 2))
            return

        @pl.when(z >= step)
        def _():
            shard = tm - 2 * step
            arrive(make(shard, 2))
            pl.when(has_up)(lambda: act(make(shard, 0)))
            act(make(shard, 2))
            if hand_over:
                act(make(shard, 3))

        @pl.when(z + step < DEPTH)
        def _():
            shard = tm + 2 * step
            arrive(make(shard, 2))
            pl.when(has_down)(lambda: act(make(shard, 1)))
            act(make(shard, 2))
            if hand_over:
                act(make(shard, 3))

    def side_round(step, make, act, arrive, hand_over):
        def one(shard):
            arrive(make(shard, 2))
            if hand_over:
                act(make(shard, 3))

        base = tm + 1 - 2 * x
        if step == 0:
            one(base)
            return
        pl.when(z >= step)(lambda: one(base - 2 * step))
        pl.when(z + step < DEPTH)(lambda: one(base + 2 * step))

    start = lambda copy: copy.start()
    sent = lambda copy: copy.wait_send()
    landed = lambda copy: copy.wait_recv()
    skip = lambda copy: None

    def w_make(tap):
        return lambda shard, way: piece(circ, tap, shard, way)

    own_copies[3].wait()
    own_copies[2].wait()
    own_copies[0].wait()
    own_copies[1].wait()
    each_tap(lambda tap: ring_round(0, w_make(tap), start, landed, True))
    ring_round(0, mix_piece, start, landed, False)
    pl.when(has_up)(lambda: halo(0, 2, up).start())
    to_mate(0, here).start()
    own_copies[4].wait()
    cot_copy(here).start()

    for lag in (1, 2):
        @pl.when(tm < lag)
        def _():
            sig[lag] = jnp.zeros_like(sig[lag])

    @pl.when(jnp.logical_not(has_up))
    def _():
        rin[1] = jnp.zeros_like(rin[1])

    for step in range(1, DEPTH):
        def body(tap):
            side_round(step - 1, w_make(tap), start, landed, True)
            ring_round(step, w_make(tap), start, landed, True)

        each_tap(body)
        ring_round(step, mix_piece, start, landed, False)
        side_round(step - 1, mix_piece, start, landed, False)
        if step == 1:
            pl.when(x == 0)(lambda: halo(0, 1, side).start())

            @pl.when(has_down)
            def _():
                halo(0, 2, side).wait_recv()
                pl.when(x == 1)(lambda: halo(2, 1, side).start())
                to_mate(2, here).start()

        if step == 2:
            @pl.when(tm >= 1)
            def _():
                halo(0, 1, side).wait_recv()
                to_mate(1, here).start()
    side_round(DEPTH - 1, mix_piece, start, landed, False)
    each_tap(lambda tap: side_round(DEPTH - 1, w_make(tap), start, landed, True))

    to_mate(0, there).wait_recv()
    for lag in (1, 2):
        pl.when(tm >= lag)(lambda: to_mate(lag, there).wait_recv())
    cot_copy(there).wait_recv()

    def other_landed(tap):
        def one(step, c):
            piece(other, tap, (tm + step) % (last + 1), 3).wait_recv()
            return c

        lax.fori_loop(1, last + 1, one, 0)

    def tiles(body):
        def one(i, c):
            body(pl.multiple_of(i * TILE, TILE))
            return c

        lax.fori_loop(0, half // TILE, one, 0)

    def early(col):
        columns = pl.ds(col, TILE)
        total = jnp.dot(sig[0], w[circ, 0, :, columns], preferred_element_type=F32)
        for tap in range(1, KERNEL_TAPS):
            total += jnp.dot(sig[tap], w[circ, tap, :, columns], preferred_element_type=F32)
        pre[circ, :, columns] = total
        backs[:, columns] = lax.dot_general(cot[...], mix[columns, :], NT, preferred_element_type=F32)

    for shard in range(last + 1):
        mix[:, shard * rows : (shard + 1) * rows] = mix_parts[shard]
    tiles(early)

    for tap in range(KERNEL_TAPS):
        other_landed(tap)

        def late(col):
            columns = pl.ds(col, TILE)
            part = jnp.dot(sig[tap], w[other, tap, :, columns], preferred_element_type=F32)
            pre[other, :, columns] = part if tap == 0 else pre[other, :, columns] + part

        tiles(late)

    def forward(col):
        columns = pl.ds(col, TILE)
        pre_f = pre[0, :, columns] + fbias_ref[:, columns]
        pre_g = pre[1, :, columns] + gbias_ref[:, columns]
        t = jnp.tanh(pre_f)
        s = jax.nn.sigmoid(pre_g)
        ts = t * s
        hidden[:, columns] = ts.astype(BF16)
        back = backs[:, columns]
        grads[:, columns] = (back * s * (1.0 - t * t)).astype(BF16)
        grads[:, pl.ds(pl.multiple_of(half + col, TILE), TILE)] = (back * ts * (1.0 - s)).astype(BF16)

    tiles(forward)

    def grad_part(tap, base, col):
        channels = pl.ds(pl.multiple_of(base + col, TILE), TILE)
        return lax.dot_general(
            grads[:, :half], w[0, tap, channels, :], NT, preferred_element_type=F32
        ) + lax.dot_general(grads[:, half:], w[1, tap, channels, :], NT, preferred_element_type=F32)

    def mix_part(base, col):
        channels = pl.ds(pl.multiple_of(base + col, TILE), TILE)
        return jnp.dot(hidden[...], mix[:, channels], preferred_element_type=F32)

    def swap(slot):
        return remote(xout.at[slot], xin.at[slot], xsend.at[slot], xrecv.at[slot], mate)

    chunk = rin.shape[1] // CHUNKS

    def back_copy(tap, part):
        piece_rows = pl.ds(part * chunk, chunk)
        return remote(
            qout.at[tap - 1, piece_rows], rin.at[tap - 1, piece_rows],
            qsend.at[tap - 1, part], qrecv.at[tap - 1, part], side if tap == 1 else down,
        )

    def all_parts(tap, act):
        for part in range(CHUNKS):
            act(back_copy(tap, part))

    side_gives = jnp.logical_or(x == 1, has_down)
    merges = jnp.logical_and(x == 1, has_down)

    def give(slot, part):
        def one(col):
            xout[slot, :, pl.ds(col, TILE)] = part(there, col).astype(BF16)

        tiles(one)
        swap(slot).start()

    def tap_part(tap):
        return lambda base, col: grad_part(tap, base, col)

    for tap in (1, 2):
        give(tap, tap_part(tap))
    for tap in (1, 2):
        def one(col):
            keep[:, pl.ds(col, TILE)] = grad_part(tap, here, col)

        tiles(one)
        swap(tap).wait_recv()
        if tap == 1:
            qout[0] = (keep[...] + xin[1].astype(F32)).astype(BF16)
            pl.when(side_gives)(lambda: all_parts(1, start))

    keep[...] = keep[...] + xin[2].astype(F32)

    @pl.when(jnp.logical_and(x == 0, has_down))
    def _():
        qout[1] = keep[...].astype(BF16)
        all_parts(2, start)

    give(3, mix_part)
    give(0, tap_part(0))

    @pl.when(merges)
    def _():
        for part in range(CHUNKS):
            back_copy(1, part).wait_recv()
            piece_rows = pl.ds(part * chunk, chunk)
            qout[1, piece_rows] = (keep[piece_rows] + rin[0, piece_rows].astype(F32)).astype(BF16)
            back_copy(2, part).start()

    def out_tile(col):
        keep[:, pl.ds(col, TILE)] = mix_part(here, col)

    tiles(out_tile)
    swap(3).wait_recv()
    out_ref[...] = (
        sig[0, :, lanes(here, half)].astype(F32) + (keep[...] + xin[3].astype(F32))
    ).astype(BF16)

    def ig_tile(col):
        keep[:, pl.ds(col, TILE)] = grad_part(0, here, col)

    tiles(ig_tile)
    swap(0).wait_recv()
    keep[...] = keep[...] + xin[0].astype(F32) + cot[:, lanes(here, half)].astype(F32)

    @pl.when(x == 0)
    def _():
        all_parts(1, landed)
        keep[...] = keep[...] + rin[0].astype(F32)

    pl.when(has_up)(lambda: all_parts(2, landed))
    ig_ref[...] = (keep[...] + rin[1].astype(F32)).astype(BF16)

    pl.when(has_up)(lambda: halo(0, 2, up).wait_send())
    pl.when(x == 0)(lambda: halo(0, 1, side).wait_send())
    pl.when(jnp.logical_and(x == 1, has_down))(lambda: halo(2, 1, side).wait_send())
    for lag in (1, 2):
        pl.when(tm >= lag)(lambda: to_mate(lag, here).wait_send())
    to_mate(0, here).wait_send()
    cot_copy(here).wait_send()
    for slot in range(4):
        swap(slot).wait_send()
    pl.when(side_gives)(lambda: all_parts(1, sent))
    pl.when(has_down)(lambda: all_parts(2, sent))

    for step in range(DEPTH):
        ring_round(step, mix_piece, sent, skip, False)

    def drain(tap):
        for step in range(DEPTH):
            ring_round(step, w_make(tap), sent, skip, True)
            side_round(step, w_make(tap), sent, skip, True)

    each_tap(drain)


def fused_device(signal, filter_weight, gate_weight, filter_bias, gate_bias, mix_weight, cotangent):
    steps, half = signal.shape
    hid = filter_weight.shape[2]
    count = lax.axis_size("tm")
    width = count * filter_weight.shape[1]
    anywhere = pl.BlockSpec(memory_space=pl.ANY)
    vmem = pl.BlockSpec(memory_space=pltpu.VMEM)
    dma = pltpu.SemaphoreType.DMA
    return pl.pallas_call(
        fused_kernel,
        out_shape=(
            jax.ShapeDtypeStruct((steps, half), BF16),
            jax.ShapeDtypeStruct((steps, half), BF16),
        ),
        in_specs=[anywhere, anywhere, anywhere, vmem, vmem, anywhere, anywhere],
        out_specs=(vmem, vmem),
        scratch_shapes=[
            pltpu.VMEM((2, KERNEL_TAPS, width, hid), BF16),
            pltpu.VMEM((hid, width), BF16),
            pltpu.VMEM((KERNEL_TAPS, steps, width), BF16),
            pltpu.VMEM((steps, width), BF16),
            pltpu.VMEM((steps, 2 * hid), BF16),
            pltpu.VMEM((steps, hid), BF16),
            pltpu.VMEM((steps, half), F32),
            pltpu.VMEM((4, steps, half), BF16),
            pltpu.VMEM((4, steps, half), BF16),
            pltpu.VMEM((2, steps, half), BF16),
            pltpu.VMEM((2, steps, half), BF16),
            dma((4, KERNEL_TAPS, count)),
            dma((2, KERNEL_TAPS, count)),
            dma((3, count)),
            dma((count,)),
            dma((3,)),
            dma((3,)),
            dma((3,)),
            dma((3,)),
            dma((1,)),
            dma((1,)),
            dma((4,)),
            dma((4,)),
            dma((2, CHUNKS)),
            dma((2, CHUNKS)),
            dma((5,)),
            pltpu.VMEM((2, steps, hid), F32),
            pltpu.VMEM((steps, hid), F32),
            pltpu.VMEM((count, hid, width // count), BF16),
        ],
        compiler_params=pltpu.CompilerParams(
            collective_id=0, has_side_effects=True, vmem_limit_bytes=56 * 1024 * 1024
        ),
    )(
        signal, filter_weight, gate_weight, filter_bias.reshape(1, -1), gate_bias.reshape(1, -1),
        mix_weight, cotangent,
    )


def solution(mesh):
    in_specs = (
        P(("grp", "tm"), "chan"),
        P(None, "tm", "chan"),
        P(None, "tm", "chan"),
        P("chan"),
        P("chan"),
        P("chan", "tm"),
        P(("grp", "tm"), "chan"),
    )
    out_specs = (P(("grp", "tm"), "chan"), P(("grp", "tm"), "chan"))
    fits = mesh.shape["tm"] == 2 * DEPTH and mesh.shape["grp"] == 2 and mesh.shape["chan"] == 2
    return jax.shard_map(
        fused_device if fits else per_device, mesh=mesh, in_specs=in_specs, out_specs=out_specs, check_vma=False
    )
```
